512 devices in a mesh: cube: 16 (over z), row: 4 (over y_lo, core), col: 8 (over y_hi, x).
Axes of the slice: x: 4, y: 4 (y_hi: 2, y_lo: 2; y = y_hi * 2 + y_lo), z: 16, core: 2. Of those that a mesh axis runs over, the one named last changes fastest.
Arguments:
- front: bfloat16 [16, 3072, 2048], P('cube', 'row', 'col'), may hold values from -6 to 6
- panel_inverse: bfloat16 [16, 1024, 256], P('cube'), may hold values from -0.16 to 0.16
- contrib: bfloat16 [16, 192, 256, 256], P('cube', ('row', 'col')), may hold values from -4 to 4
- pattern: int32 [16, 192, 2], P('cube', ('row', 'col')), may hold values from -1 to 11, as said below
- front_map: int32 [16, 12], P('cube'), may hold values from 0 to 11, as said below
Outputs:
- factored: bfloat16 [16, 3072, 2048], P('cube', 'row', 'col')
The draws below stay inside these ranges and needn't reach their ends.
Inputs may be any that keep to these rules, and one draw needn't show every extreme that they name: `pattern`: each slot holds (-1, -1) when empty, else two child block indices. For a live slot of a device with col index q, front_map of its cube maps the column index to a block below 8 with residue q mod 8. Of one device's live slots at most 3 map to front block rows of one residue mod 4; in every cube and col index some residue receives exactly 3 from every device of that col index. `front_map`: for each cube a permutation of the block indices that maps blocks below 8 to blocks below 8 with the same residue mod 8.
All inputs are finite; a program needn't handle non-finite values.
Results may differ from the reference program's by a relative error of at most 0.0055.
Values may be sent and summed in bfloat16 or wider, within the bound.
A program may use at most 64 MiB of HBM per device.

```python
import math
import jax
import jax.numpy as jnp
from jax import lax

BLK = 256
ROWB = 12
KB = 8
PANELS = 4
SLOTS = 6
CAP = 3
ROWS = 3072
COLS = 2048
N_CUBE = 16
N_ROW = 4
N_COL = 8


def shared_map(key):
    key = jax.random.fold_in(key, 11)
    per_class = KB // N_COL
    subkeys = jax.random.split(key, N_CUBE * N_COL + N_CUBE)
    lower_part = jax.vmap(lambda subkey: jax.random.permutation(subkey, per_class))(subkeys[:N_CUBE * N_COL])
    lower_part = lower_part.reshape(N_CUBE, N_COL, per_class).astype(jnp.int32)
    upper_part = jax.vmap(lambda subkey: jax.random.permutation(subkey, ROWB - KB))(subkeys[N_CUBE * N_COL:])
    classes = jnp.arange(N_COL, dtype=jnp.int32)
    lower_part = classes[None, :, None] + N_COL * lower_part
    lower_part = lower_part.transpose(0, 2, 1).reshape(N_CUBE, KB)
    return jnp.concatenate([lower_part, KB + upper_part.astype(jnp.int32)], axis=1).astype(jnp.int32)


def draw_front_map(key, part):
    return shared_map(key)


def draw_pattern(key, part):
    mapping = shared_map(key)
    key = jax.random.fold_in(key, 5)
    inverse = jax.vmap(lambda mapped: jnp.zeros((ROWB,), jnp.int32).at[mapped].set(jnp.arange(ROWB, dtype=jnp.int32)))(mapping)
    devices = N_ROW * N_COL
    subkeys = jax.random.split(key, 6)
    shape = (N_CUBE, devices, SLOTS)
    hottest = jax.random.randint(subkeys[0], (N_CUBE, N_COL), 0, N_ROW)
    col_of = jnp.arange(devices, dtype=jnp.int32) % N_COL
    hot_device = hottest[:, col_of]
    slot_index = jnp.arange(SLOTS, dtype=jnp.int32)
    others = (hot_device[:, :, None] + 1 + jax.random.randint(subkeys[1], shape, 0, N_ROW - 1)) % N_ROW
    target_row = jnp.where(slot_index[None, None, :] < CAP, hot_device[:, :, None], others)
    alive = (slot_index < CAP)[None, None, :] | (jax.random.randint(subkeys[2], shape, 0, 2) == 1)
    front_row = target_row + N_ROW * jax.random.randint(subkeys[3], shape, 0, ROWB // N_ROW)
    front_col = col_of[None, :, None] + N_COL * jax.random.randint(subkeys[4], shape, 0, KB // N_COL)
    cube_index = jnp.arange(N_CUBE, dtype=jnp.int32)[:, None, None]
    child_row = jnp.where(alive, inverse[cube_index, front_row], -1)
    child_col = jnp.where(alive, inverse[cube_index, front_col], -1)
    pairs = jnp.stack([child_row, child_col], axis=-1)
    order_keys = jax.random.split(subkeys[5], N_CUBE * devices)
    orders = jax.vmap(lambda subkey: jax.random.permutation(subkey, SLOTS))(order_keys).reshape(N_CUBE, devices, SLOTS)
    pairs = jnp.take_along_axis(pairs, orders[:, :, :, None], axis=2)
    return pairs.reshape(N_CUBE, devices * SLOTS, 2).astype(jnp.int32)


def draw_panel_inverse(key, part):
    key = jax.random.fold_in(key, 17)
    subkeys = jax.random.split(key, 3)
    shape = (N_CUBE, PANELS, BLK, BLK)
    diag_shape = (N_CUBE, PANELS, BLK)
    signs = (2 * jax.random.randint(subkeys[0], diag_shape, 0, 2) - 1).astype(jnp.float32)
    magnitude = jax.random.uniform(subkeys[1], diag_shape, jnp.float32, 1.6, 2.0)
    spread = jnp.clip(jax.random.normal(subkeys[2], shape, jnp.float32), -4.0, 4.0) * 0.45
    offdiag = spread / math.sqrt(BLK)
    row_ids = jnp.arange(BLK, dtype=jnp.int32)[:, None]
    col_ids = jnp.arange(BLK, dtype=jnp.int32)[None, :]
    diagonal = (signs * magnitude)[:, :, :, None]
    matrix = jnp.where(row_ids == col_ids, diagonal, offdiag)
    return (0.067 * matrix).reshape(N_CUBE, PANELS * BLK, BLK).astype(jnp.bfloat16)


def shard_levels(stream_key, shape, shards, least, top_value):
    def one(position, blocks):
        heights = jax.random.uniform(jax.random.fold_in(jax.random.fold_in(stream_key, 6), position), (blocks,), jnp.float32, least / len(shards), top_value / len(shards))
        return jnp.repeat(jnp.exp(heights), shape[position] // blocks).reshape((-1,) + (1,) * (len(shape) - position - 1))

    loudness = one(*shards[0])
    for cut in shards[1:]:
        loudness = loudness * one(*cut)
    return loudness


def noise(stream_key, dims, width, bound, shards=(), kind=jnp.bfloat16):
    gain = shard_levels(stream_key, dims, shards, -0.22, 0.18) if shards else 1.0
    entries = jax.random.normal(stream_key, dims, jnp.float32) * width * gain
    return jnp.minimum(jnp.maximum(entries, -bound), bound).astype(kind)


def setup_inputs(seed: int = 0) -> dict:
    splits = jax.random.split(jax.random.key(seed), 6)
    return {
        "front": noise(splits[0], (N_CUBE, ROWS, COLS), 1.0, 6.0, ((0, 16), (1, 4), (2, 8))),
        "panel_inverse": draw_panel_inverse(jax.random.fold_in(splits[5], 71), 0),
        "contrib": noise(splits[2], (N_CUBE, N_ROW * N_COL * SLOTS, BLK, BLK), 0.5, 4.0, ((0, 16), (1, 32))),
        "pattern": draw_pattern(jax.random.fold_in(splits[5], 71), 0),
        "front_map": draw_front_map(jax.random.fold_in(splits[5], 71), 0),
    }


def from_stored(stored, groups):
    count = stored.shape[0] // (groups * BLK)
    return stored.reshape(groups, count, BLK, stored.shape[1]).transpose(1, 0, 2, 3).reshape(stored.shape)


def to_stored(matrix, groups):
    count = matrix.shape[0] // (groups * BLK)
    return matrix.reshape(count, groups, BLK, matrix.shape[1]).transpose(1, 0, 2, 3).reshape(matrix.shape)


def reference(front, panel_inverse, contrib, pattern, front_map):
    half_cubes = N_CUBE // 2

    def one_cube(index):
        partner = jnp.bitwise_xor(index, half_cubes)
        stored = front[index].astype(jnp.float32)
        matrix = from_stored(from_stored(stored, N_ROW).T, N_COL).T
        values = contrib[partner].astype(jnp.float32)
        slot_pairs = pattern[partner]
        mapping = front_map[partner]
        is_live = slot_pairs[:, 0] >= 0
        row_blocks = jnp.where(is_live, mapping[jnp.maximum(slot_pairs[:, 0], 0)], ROWB).astype(jnp.int32)
        col_blocks = mapping[jnp.maximum(slot_pairs[:, 1], 0)].astype(jnp.int32)
        blocks = matrix.reshape(ROWB, BLK, KB, BLK)
        blocks = blocks.at[row_blocks, :, col_blocks, :].add(values, mode="drop")
        matrix = blocks.reshape(ROWB * BLK, KB * BLK)
        row_index = jnp.arange(ROWB * BLK, dtype=jnp.int32) // BLK
        for step in range(PANELS):
            weight = panel_inverse[index, step * BLK:(step + 1) * BLK]
            column = matrix[:, step * BLK:(step + 1) * BLK].astype(jnp.bfloat16)
            product = jnp.dot(column, weight, preferred_element_type=jnp.float32)
            panel = jnp.where((row_index > step)[:, None], product, jnp.float32(0.0)).astype(jnp.bfloat16)
            lower = (step + 1) * BLK
            update = jnp.dot(panel[lower:], panel[lower:KB * BLK].T, preferred_element_type=jnp.float32)
            matrix = matrix.at[lower:, lower:].add(-update)
            matrix = matrix.at[:, step * BLK:lower].set(panel.astype(jnp.float32))
        result = to_stored(to_stored(matrix, N_ROW).T, N_COL).T
        return result.astype(jnp.bfloat16)

    return lax.map(one_cube, jnp.arange(N_CUBE, dtype=jnp.int32))
```

```python
import jax
import jax.numpy as jnp
from jax import lax
from jax.experimental import pallas as pl
from jax.experimental.pallas import tpu as pltpu
from jax.sharding import PartitionSpec as P

MESH = pl.DeviceIdType.MESH
PANELS = 4
F32 = jnp.float32
BF16 = jnp.bfloat16
OWN_ROWS = 1024
LEAD_ROWS = 1280
HOPS = 8


def dot_t(a, b):
    return lax.dot_general(a, b, (((1,), (1,)), ((), ())), preferred_element_type=F32)


def kernel(
    front, winv, contrib, pat, fmap, out,
    cv, fv, wv, sc, cr, own, ys, yr, xs, z, fx, a_st, l_st, part, ox, ob,
    lsem, csend, crecv, ysend, yrecv, xsend, xrecv, fsend, frecv, zsend, zrecv,
    gsend, grecv, tsend, trecv, usend, urecv, qsend, qrecv, vsend, vrecv, osend, orecv,
):
    cube = lax.axis_index("cube")
    row = lax.axis_index("row")
    col = lax.axis_index("col")
    cubes = lax.axis_size("cube")
    core = row % 2
    ylo = row // 2
    half = col // 4
    xpos = col % 4

    def at_row_col(r, c):
        return {"row": r, "col": c}

    core_peer = at_row_col(row ^ 1, col)
    y_peers = {m: at_row_col(row ^ (2 * (m & 1)), col ^ (4 * (m >> 1))) for m in (1, 2, 3)}
    x_peers = {m: at_row_col(row, col ^ m) for m in (1, 2, 3)}
    z_peers = [{"cube": (cube + 1) % cubes}, {"cube": (cube + cubes - 1) % cubes}]

    def remote(src, dst, ssem, rsem, peer):
        return pltpu.make_async_remote_copy(src, dst, ssem, rsem, device_id=peer, device_id_type=MESH)

    loads = [
        pltpu.make_async_copy(contrib, cv, lsem.at[0]),
        pltpu.make_async_copy(front, fv, lsem.at[1]),
        pltpu.make_async_copy(winv, wv, lsem.at[2]),
    ]
    for c in loads:
        c.start()

    barrier = pltpu.get_barrier_semaphore()
    peers = [core_peer, *y_peers.values(), *x_peers.values(), *z_peers]
    for p in peers:
        pl.semaphore_signal(barrier, 1, device_id=p, device_id_type=MESH)
    targets = []
    for s in range(6):
        child = pat[s, 0]
        targets.append(jnp.where(child >= 0, fmap[jnp.maximum(child, 0)], -1))
    loads[0].wait()

    def c_copy(i):
        return remote(sc.at[i], cr.at[i], csend.at[i], crecv.at[i], core_peer)

    for i in range(3):
        def masks(y, c):
            block = y * 2 + c + 4 * i
            return [(t == block).astype(F32) for t in targets]

        away = [masks(y, 1 - core) for y in range(2)]
        stay = [masks(y, core) for y in range(2)]

        def tile(t, carry):
            rows = pl.ds(pl.multiple_of(t * 32, 32), 32)
            vals = [cv[s, rows, :].astype(F32) for s in range(6)]

            def total(ms):
                acc = vals[0] * ms[0]
                for v, m in zip(vals[1:], ms[1:]):
                    acc = acc + v * m
                return acc

            for y in range(2):
                sc[i, y, rows, :] = total(away[y]).astype(BF16)
            for y in range(2):
                own[i, y, rows, :] = total(stay[y])
            return carry

        lax.fori_loop(0, 8, tile, 0)
        if i == 0:
            pl.semaphore_wait(barrier, len(peers))
        c_copy(i).start()

    def y_copy(i):
        return remote(ys.at[i], yr.at[i], ysend.at[i], yrecv.at[i], y_peers[1])

    for i in range(3):
        c_copy(i).wait_recv()
        ys[i] = (own[i, 1 - ylo] + cr[i, 1 - ylo].astype(F32)).astype(BF16)
        y_copy(i).start()
        own[i, ylo] = own[i, ylo] + cr[i, ylo].astype(F32)

    mine = pl.ds(pl.multiple_of(half * 128, 128), 128)
    theirs = pl.ds(pl.multiple_of((1 - half) * 128, 128), 128)

    def x_copy(i):
        return remote(xs.at[i], z.at[half, 0, i], xsend.at[i], xrecv.at[i], y_peers[2])

    def x_arrival(i):
        return remote(xs.at[i], z.at[1 - half, 0, i], xsend.at[i], xrecv.at[i], y_peers[2])

    for i in range(3):
        y_copy(i).wait_recv()
        xs[i] = (own[i, ylo, theirs, :] + yr[i, theirs, :].astype(F32)).astype(BF16)
        x_copy(i).start()
        z[half, 0, i] = (own[i, ylo, mine, :] + yr[i, mine, :].astype(F32)).astype(BF16)

    def z_copy(j, s, i, d):
        rows = pl.ds(d * 64, 64)
        return remote(
            z.at[j, s, i, rows], z.at[j, s + 1, i, rows],
            zsend.at[j, s, i, d], zrecv.at[j, s, i, d], z_peers[d],
        )

    for i in range(3):
        x_arrival(i).wait_recv()
        for d in range(2):
            z_copy(0, 0, i, d).start()

    loads[1].wait()
    f_copy = remote(fv.at[:, theirs], fx, fsend, frecv, y_peers[2])
    f_copy.start()

    def z_step(j, s):
        for i in range(3):
            for d in range(2):
                z_copy(j, s - 1, i, d).wait_recv()
                z_copy(j, s, i, d).start()

    def z_body(s, carry):
        z_step(0, s)
        return carry

    lax.fori_loop(1, HOPS, z_body, 0)
    for i in range(3):
        for d in range(2):
            z_copy(1, 0, i, d).start()

    top = pl.multiple_of(row * 256 + half * 128, 128)
    f_copy.wait_recv()
    first = half == 0

    def g_copy(m, part_no):
        rows = pl.ds(top, 128) if part_no == 0 else pl.ds(OWN_ROWS, 256)
        ref = a_st.at[xpos, rows]
        return remote(ref, ref, gsend.at[m - 1, part_no], grecv.at[m - 1, part_no], x_peers[m])

    def g_arrival(m, part_no):
        rows = pl.ds(top, 128) if part_no == 0 else pl.ds(OWN_ROWS, 256)
        ref = a_st.at[xpos ^ m, rows]
        return remote(ref, ref, gsend.at[m - 1, part_no], grecv.at[m - 1, part_no], x_peers[m])

    for i in range(3):
        for d in range(2):
            z_copy(0, HOPS - 1, i, d).wait_recv()
        base = jnp.where(first, fv[i, mine, :].astype(F32), fx[i].astype(F32))
        value = (base + z[0, HOPS, i].astype(F32)).astype(BF16)
        if i == 0:
            a_st[xpos, pl.ds(top, 128), :] = value
            for m in (1, 2, 3):
                g_copy(m, 0).start()
        else:
            a_st[xpos, pl.ds(OWN_ROWS + (i - 1) * 128, 128), :] = value
    for m in (1, 2, 3):
        g_copy(m, 1).start()

    for k in range(PANELS):
        @pl.when(row <= k)
        def _():
            l_st[k, pl.ds(top, 128), :] = jnp.zeros((128, 256), BF16)

    z_step(1, 1)
    z_step(1, 2)

    def tri_place(r, h):
        return a_st.at[pl.ds(0, 3), pl.ds(pl.multiple_of(r * 256 + h * 128, 128), 128)]

    def lead_place(h):
        return a_st.at[:, pl.ds(pl.multiple_of(LEAD_ROWS + h * 128, 128), 128)]

    def owner(m):
        return row ^ (2 * (m & 1)), half ^ (m >> 1)

    def t_copy(m):
        ref = tri_place(row, half)
        return remote(ref, ref, tsend.at[m - 1], trecv.at[m - 1], y_peers[m])

    def t_arrival(m):
        ref = tri_place(*owner(m))
        return remote(ref, ref, tsend.at[m - 1], trecv.at[m - 1], y_peers[m])

    def u_copy(m):
        ref = tri_place(*owner(m))
        return remote(ref, ref, usend.at[m], urecv.at[m], core_peer)

    def u_arrival(m):
        r, h = owner(m)
        ref = tri_place(r ^ 1, h)
        return remote(ref, ref, usend.at[m], urecv.at[m], core_peer)

    def q_copy(m):
        return remote(lead_place(half), lead_place(half), qsend.at[m - 1], qrecv.at[m - 1], y_peers[m])

    def q_arrival(m):
        ref = lead_place(owner(m)[1])
        return remote(ref, ref, qsend.at[m - 1], qrecv.at[m - 1], y_peers[m])

    def v_copy(m):
        ref = lead_place(owner(m)[1])
        return remote(ref, ref, vsend.at[m], vrecv.at[m], core_peer)

    for m in (1, 2, 3):
        for part_no in range(2):
            g_arrival(m, part_no).wait_recv()
    for m in (1, 2, 3):
        t_copy(m).start()
    u_copy(0).start()

    @pl.when(row == xpos)
    def _():
        for k in range(4):
            a_st[k, pl.ds(pl.multiple_of(LEAD_ROWS + half * 128, 128), 128), :] = a_st[k, pl.ds(OWN_ROWS, 128), :]
        for m in (1, 2, 3):
            q_copy(m).start()
        v_copy(0).start()

    z_step(1, 3)
    z_step(1, 4)

    for m in (1, 2, 3):
        t_arrival(m).wait_recv()
        u_copy(m).start()

        @pl.when(owner(m)[0] == xpos)
        def _():
            q_arrival(m).wait_recv()
            v_copy(m).start()

    z_step(1, 5)

    for m in range(4):
        u_arrival(m).wait_recv()

        @pl.when((owner(m)[0] ^ 1) == xpos)
        def _():
            v_copy(m).wait_recv()

    loads[2].wait()

    def panel(k, b):
        rows = pl.ds(b * 256, 256)
        acc = a_st[k, rows, :].astype(F32)
        for m in range(k):
            acc = acc - dot_t(l_st[m, rows, :], l_st[m, pl.ds(k * 256, 256), :])
        weight = wv[pl.ds(k * 256, 256), :]
        l_st[k, rows, :] = jnp.dot(acc.astype(BF16), weight, preferred_element_type=F32).astype(BF16)

    for k in range(2):
        for b in range(k + 1, 6):
            panel(k, b)
    z_step(1, 6)
    for k in range(2, 4):
        for b in range(k + 1, 6):
            panel(k, b)
    z_step(1, 7)

    def rows_of(i):
        return pl.ds(top, 128) if i == 0 else pl.ds(OWN_ROWS + (i - 1) * 128, 128)

    for i in range(3):
        acc = jnp.where(first, fx[i].astype(F32), fv[i, mine, :].astype(F32))
        for k in range(PANELS):
            acc = acc - dot_t(l_st[k, rows_of(i), :], l_st[k, pl.ds(LEAD_ROWS, 256), :])
        part[i] = acc

    def o_copy(i):
        return remote(ox.at[i], ob.at[i, mine], osend.at[i], orecv.at[i], y_peers[2])

    def o_arrival(i):
        return remote(ox.at[i], ob.at[i, theirs], osend.at[i], orecv.at[i], y_peers[2])

    for i in range(3):
        for d in range(2):
            z_copy(1, HOPS - 1, i, d).wait_recv()
        late = (part[i] + z[1, HOPS, i].astype(F32)).astype(BF16)
        early = l_st[xpos, rows_of(i), :]
        ox[i] = jnp.where(first, late, early)
        o_copy(i).start()
        ob[i, mine, :] = jnp.where(first, early, late)
    for i in range(3):
        o_arrival(i).wait_recv()
    store = pltpu.make_async_copy(ob, out, lsem.at[3])
    store.start()

    for i in range(3):
        c_copy(i).wait_send()
        y_copy(i).wait_send()
        x_copy(i).wait_send()
        o_copy(i).wait_send()
    f_copy.wait_send()
    for m in (1, 2, 3):
        for part_no in range(2):
            g_copy(m, part_no).wait_send()
        t_copy(m).wait_send()
    for m in range(4):
        u_copy(m).wait_send()

        @pl.when(owner(m)[0] == xpos)
        def _():
            v_copy(m).wait_send()

    @pl.when(row == xpos)
    def _():
        for m in (1, 2, 3):
            q_copy(m).wait_send()

    def drain(s, carry):
        for j in range(2):
            for i in range(3):
                for d in range(2):
                    z_copy(j, s, i, d).wait_send()
        return carry

    lax.fori_loop(0, HOPS, drain, 0)
    store.wait()


def shards(front, panel_inverse, contrib, pattern, front_map):
    hbm = pl.BlockSpec(memory_space=pl.ANY)
    smem = pl.BlockSpec(memory_space=pltpu.SMEM)

    def vmem(*shape, dtype=BF16):
        return pltpu.VMEM(shape, dtype)

    def dma(*shape):
        return pltpu.SemaphoreType.DMA(shape)

    out = pl.pallas_call(
        kernel,
        out_shape=jax.ShapeDtypeStruct((3, 256, 256), BF16),
        in_specs=[hbm, hbm, hbm, smem, smem],
        out_specs=hbm,
        scratch_shapes=[
            vmem(6, 256, 256),
            vmem(3, 256, 256),
            vmem(1024, 256),
            vmem(3, 2, 256, 256),
            vmem(3, 2, 256, 256),
            vmem(3, 2, 256, 256, dtype=F32),
            vmem(3, 256, 256),
            vmem(3, 256, 256),
            vmem(3, 128, 256),
            vmem(2, HOPS + 1, 3, 128, 256),
            vmem(3, 128, 256),
            vmem(4, 1536, 256),
            vmem(4, 1536, 256),
            vmem(3, 128, 256, dtype=F32),
            vmem(3, 128, 256),
            vmem(3, 256, 256),
            dma(4),
            dma(3), dma(3), dma(3), dma(3), dma(3), dma(3),
            pltpu.SemaphoreType.DMA, pltpu.SemaphoreType.DMA,
            dma(2, HOPS, 3, 2), dma(2, HOPS, 3, 2),
            dma(3, 2), dma(3, 2),
            dma(3), dma(3), dma(4), dma(4),
            dma(3), dma(3), dma(4), dma(4),
            dma(3), dma(3),
        ],
        compiler_params=pltpu.CompilerParams(
            collective_id=0, has_side_effects=True, vmem_limit_bytes=60 * 2**20
        ),
        name="extend_add_eliminate",
    )(front.reshape(3, 256, 256), panel_inverse[0], contrib[0], pattern[0], front_map[0])
    return out.reshape(1, 768, 256)


def solution(mesh):
    in_specs = (
        P("cube", "row", "col"),
        P("cube", None, None),
        P("cube", ("row", "col"), None, None),
        P("cube", ("row", "col"), None),
        P("cube", None),
    )
    out_specs = P("cube", "row", "col")
    return jax.shard_map(shards, mesh=mesh, in_specs=in_specs, out_specs=out_specs, check_vma=False)
```

```python
import jax
import jax.numpy as jnp
from jax import lax
from jax.experimental import pallas as pl
from jax.experimental.pallas import tpu as pltpu
from jax.sharding import PartitionSpec as P

MESH = pl.DeviceIdType.MESH
PANELS = 4
F32 = jnp.float32
BF16 = jnp.bfloat16
OWN_ROWS = 1024
LEAD_ROWS = 1280


def dot_t(a, b):
    return lax.dot_general(a, b, (((1,), (1,)), ((), ())), preferred_element_type=F32)


def kernel(
    front, winv, contrib, pat, fmap, out,
    cv, fv, wv, sc, cr, own, kept, ys, yr, zs, zr, fx, a_st, l_st, part, ox, ob,
    lsem, csend, crecv, ysend, yrecv, fsend, frecv, zsend, zrecv,
    gsend, grecv, tsend, trecv, usend, urecv, qsend, qrecv, vsend, vrecv, osend, orecv,
):
    cube = lax.axis_index("cube")
    row = lax.axis_index("row")
    col = lax.axis_index("col")
    cubes = lax.axis_size("cube")
    core = row % 2
    ylo = row // 2
    half = col // 4
    xpos = col % 4

    def at_row_col(r, c):
        return {"row": r, "col": c}

    core_peer = at_row_col(row ^ 1, col)
    y_peers = {m: at_row_col(row ^ (2 * (m & 1)), col ^ (4 * (m >> 1))) for m in (1, 2, 3)}
    x_peers = {m: at_row_col(row, col ^ m) for m in (1, 2, 3)}
    z_peer = {"cube": (cube + cubes // 2) % cubes}

    def remote(src, dst, ssem, rsem, peer):
        return pltpu.make_async_remote_copy(src, dst, ssem, rsem, device_id=peer, device_id_type=MESH)

    barrier = pltpu.get_barrier_semaphore()
    peers = [z_peer, core_peer, *y_peers.values(), *x_peers.values()]
    for p in peers:
        pl.semaphore_signal(barrier, 1, device_id=p, device_id_type=MESH)
    loads = [
        pltpu.make_async_copy(contrib, cv, lsem.at[0]),
        pltpu.make_async_copy(front, fv, lsem.at[1]),
        pltpu.make_async_copy(winv, wv, lsem.at[2]),
    ]
    for c in loads:
        c.start()

    targets = []
    for s in range(6):
        child = pat[0, s]
        targets.append(jnp.where(child >= 0, fmap[jnp.maximum(child, 0)], -1))
    loads[0].wait()

    def c_copy(i):
        return remote(sc.at[i], cr.at[i], csend.at[i], crecv.at[i], core_peer)

    for i in range(3):
        def masks(y, c):
            block = y * 2 + c + 4 * i
            return [(t == block).astype(F32) for t in targets]

        away = [masks(y, 1 - core) for y in range(2)]
        stay = [masks(y, core) for y in range(2)]

        def tile(t, carry):
            rows = pl.ds(pl.multiple_of(t * 32, 32), 32)
            vals = [cv[s, rows, :].astype(F32) for s in range(6)]

            def total(ms):
                acc = vals[0] * ms[0]
                for v, m in zip(vals[1:], ms[1:]):
                    acc = acc + v * m
                return acc

            for y in range(2):
                sc[i, y, rows, :] = total(away[y]).astype(BF16)
            for y in range(2):
                own[i, y, rows, :] = total(stay[y])
            return carry

        lax.fori_loop(0, 8, tile, 0)

    pl.semaphore_wait(barrier, len(peers))
    for i in range(3):
        c_copy(i).start()

    own_half = pl.ds(pl.multiple_of(half * 128, 128), 128)
    far_half = pl.ds(pl.multiple_of((1 - half) * 128, 128), 128)

    def y_copy(m, i):
        return remote(ys.at[m - 1, i], yr.at[m - 1, i], ysend.at[m - 1, i], yrecv.at[m - 1, i], y_peers[m])

    def both(i, y, rows):
        return own[i, y, rows, :] + cr[i, y, rows, :].astype(F32)

    for i in range(3):
        c_copy(i).wait_recv()
        ys[2, i] = both(i, 1 - ylo, far_half).astype(BF16)
        y_copy(3, i).start()
        ys[1, i] = both(i, ylo, far_half).astype(BF16)
        y_copy(2, i).start()
        ys[0, i] = both(i, 1 - ylo, own_half).astype(BF16)
        y_copy(1, i).start()
        kept[i] = both(i, ylo, own_half)

    def z_copy(j, i):
        return remote(zs.at[j, i], zr.at[j, i], zsend.at[j, i], zrecv.at[j, i], z_peer)

    for i in range(3):
        for m in (1, 2, 3):
            y_copy(m, i).wait_recv()
        zs[half, i] = (kept[i] + yr[0, i].astype(F32)).astype(BF16)
        zs[1 - half, i] = (yr[1, i].astype(F32) + yr[2, i].astype(F32)).astype(BF16)
        z_copy(0, i).start()

    loads[1].wait()
    f_copy = remote(fv.at[:, far_half], fx, fsend, frecv, y_peers[2])
    f_copy.start()

    top = pl.multiple_of(row * 256 + half * 128, 128)

    def rows_of(i):
        return pl.ds(top, 128) if i == 0 else pl.ds(OWN_ROWS + (i - 1) * 128, 128)

    for k in range(PANELS):
        @pl.when(row <= k)
        def _():
            l_st[k, rows_of(0), :] = jnp.zeros((128, 256), BF16)

    f_copy.wait_recv()
    first = half == 0

    def g_copy(m, i):
        ref = a_st.at[xpos, rows_of(i)]
        return remote(ref, ref, gsend.at[m - 1, i], grecv.at[m - 1, i], x_peers[m])

    def g_arrival(m, i):
        ref = a_st.at[xpos ^ m, rows_of(i)]
        return remote(ref, ref, gsend.at[m - 1, i], grecv.at[m - 1, i], x_peers[m])

    def critical(i):
        z_copy(0, i).wait_recv()
        base = jnp.where(first, fv[i, own_half, :].astype(F32), fx[i].astype(F32))
        a_st[xpos, rows_of(i), :] = (base + zr[0, i].astype(F32)).astype(BF16)

    def owner(m):
        return row ^ (2 * (m & 1)), half ^ (m >> 1)

    def tri_place(k, r, h):
        return a_st.at[k, pl.ds(pl.multiple_of(r * 256 + h * 128, 128), 128)]

    def lead_place(h):
        return a_st.at[:, pl.ds(pl.multiple_of(LEAD_ROWS + h * 128, 128), 128)]

    def t_copy(m, k):
        ref = tri_place(k, row, half)
        return remote(ref, ref, tsend.at[m - 1, k], trecv.at[m - 1, k], y_peers[m])

    def t_arrival(m, k):
        ref = tri_place(k, *owner(m))
        return remote(ref, ref, tsend.at[m - 1, k], trecv.at[m - 1, k], y_peers[m])

    def u_copy(m, k):
        ref = tri_place(k, *owner(m))
        return remote(ref, ref, usend.at[m, k], urecv.at[m, k], core_peer)

    def u_arrival(m, k):
        r, h = owner(m)
        ref = tri_place(k, r ^ 1, h)
        return remote(ref, ref, usend.at[m, k], urecv.at[m, k], core_peer)

    def q_copy(m):
        return remote(lead_place(half), lead_place(half), qsend.at[m - 1], qrecv.at[m - 1], y_peers[m])

    def q_arrival(m):
        ref = lead_place(owner(m)[1])
        return remote(ref, ref, qsend.at[m - 1], qrecv.at[m - 1], y_peers[m])

    def v_copy(m):
        ref = lead_place(owner(m)[1])
        return remote(ref, ref, vsend.at[m], vrecv.at[m], core_peer)

    def each(count, body):
        def step(k, carry):
            body(k)
            return carry

        lax.fori_loop(0, count, step, 0)

    critical(0)

    @pl.when(row > xpos)
    def _():
        for m in (1, 2, 3):
            g_copy(m, 0).start()

    z_copy(1, 0).start()
    critical(1)
    for m in (1, 2, 3):
        g_copy(m, 1).start()
    z_copy(1, 1).start()
    for m in (1, 2, 3):
        @pl.when(row > (xpos ^ m))
        def _():
            g_arrival(m, 0).wait_recv()

    def send_tri(k):
        for m in (3, 1, 2):
            t_copy(m, k).start()
        u_copy(0, k).start()

    each(row, send_tri)

    for m in (1, 2, 3):
        g_arrival(m, 1).wait_recv()

    @pl.when(row == xpos)
    def _():
        for k in range(4):
            a_st[k, pl.ds(pl.multiple_of(LEAD_ROWS + half * 128, 128), 128), :] = a_st[k, rows_of(1), :]
        for m in (3, 1, 2):
            q_copy(m).start()
        v_copy(0).start()

    critical(2)
    for m in (1, 2, 3):
        g_copy(m, 2).start()
    z_copy(1, 2).start()

    for m in (1, 3, 2):
        def relay_tri(k):
            t_arrival(m, k).wait_recv()
            u_copy(m, k).start()

        each(owner(m)[0], relay_tri)
    for m in (1, 3, 2):
        @pl.when(owner(m)[0] == xpos)
        def _():
            q_arrival(m).wait_recv()
            v_copy(m).start()

    for m in range(4):
        each(owner(m)[0] ^ 1, lambda k: u_arrival(m, k).wait_recv())
    loads[2].wait()

    def panel(k, b):
        rows = pl.ds(b * 256, 256)
        acc = a_st[k, rows, :].astype(F32)
        for m in range(k):
            acc = acc - dot_t(l_st[m, rows, :], l_st[m, pl.ds(k * 256, 256), :])
        weight = wv[pl.ds(k * 256, 256), :]
        l_st[k, rows, :] = jnp.dot(acc.astype(BF16), weight, preferred_element_type=F32).astype(BF16)

    for k in range(3):
        for b in range(k + 1, 4):
            panel(k, b)
    for m in (1, 2, 3):
        g_arrival(m, 2).wait_recv()
    for k in range(PANELS):
        panel(k, 4)
    for m in range(4):
        @pl.when((owner(m)[0] ^ 1) == xpos)
        def _():
            v_copy(m).wait_recv()

    for k in range(PANELS):
        panel(k, 5)

    for i in range(3):
        acc = jnp.where(first, fx[i].astype(F32), fv[i, own_half, :].astype(F32))
        for k in range(PANELS):
            acc = acc - dot_t(l_st[k, rows_of(i), :], l_st[k, pl.ds(LEAD_ROWS, 256), :])
        part[i] = acc

    def o_copy(i):
        return remote(ox.at[i], ob.at[i, own_half], osend.at[i], orecv.at[i], y_peers[2])

    def o_arrival(i):
        return remote(ox.at[i], ob.at[i, far_half], osend.at[i], orecv.at[i], y_peers[2])

    for i in range(3):
        z_copy(1, i).wait_recv()
        late = (part[i] + zr[1, i].astype(F32)).astype(BF16)
        early = l_st[xpos, rows_of(i), :]
        ox[i] = jnp.where(first, late, early)
        o_copy(i).start()
        ob[i, own_half, :] = jnp.where(first, early, late)
    for i in range(3):
        o_arrival(i).wait_recv()
    store = pltpu.make_async_copy(ob, out, lsem.at[3])
    store.start()

    f_copy.wait_send()
    for i in range(3):
        c_copy(i).wait_send()
        o_copy(i).wait_send()
        for m in (1, 2, 3):
            y_copy(m, i).wait_send()
            if i:
                g_copy(m, i).wait_send()

    @pl.when(row > xpos)
    def _():
        for m in (1, 2, 3):
            g_copy(m, 0).wait_send()

    def drain_tri(k):
        for m in (1, 2, 3):
            t_copy(m, k).wait_send()

    each(row, drain_tri)
    for m in range(4):
        each(owner(m)[0], lambda k: u_copy(m, k).wait_send())

        @pl.when(owner(m)[0] == xpos)
        def _():
            v_copy(m).wait_send()

    @pl.when(row == xpos)
    def _():
        for m in (1, 2, 3):
            q_copy(m).wait_send()

    for i in range(3):
        for j in range(2):
            z_copy(j, i).wait_send()
    store.wait()


def shards(front, panel_inverse, contrib, pattern, front_map):
    hbm = pl.BlockSpec(memory_space=pl.ANY)
    smem = pl.BlockSpec(memory_space=pltpu.SMEM)

    def vmem(*shape, dtype=BF16):
        return pltpu.VMEM(shape, dtype)

    def dma(*shape):
        return pltpu.SemaphoreType.DMA(shape)

    out = pl.pallas_call(
        kernel,
        out_shape=jax.ShapeDtypeStruct((3, 256, 256), BF16),
        in_specs=[hbm, hbm, hbm, smem, smem],
        out_specs=hbm,
        scratch_shapes=[
            vmem(6, 256, 256),
            vmem(3, 256, 256),
            vmem(1024, 256),
            vmem(3, 2, 256, 256),
            vmem(3, 2, 256, 256),
            vmem(3, 2, 256, 256, dtype=F32),
            vmem(3, 128, 256, dtype=F32),
            vmem(3, 3, 128, 256),
            vmem(3, 3, 128, 256),
            vmem(2, 3, 128, 256),
            vmem(2, 3, 128, 256),
            vmem(3, 128, 256),
            vmem(4, 1536, 256),
            vmem(4, 1536, 256),
            vmem(3, 128, 256, dtype=F32),
            vmem(3, 128, 256),
            vmem(3, 256, 256),
            dma(4),
            dma(3), dma(3), dma(3, 3), dma(3, 3),
            pltpu.SemaphoreType.DMA, pltpu.SemaphoreType.DMA,
            dma(2, 3), dma(2, 3),
            dma(3, 3), dma(3, 3),
            dma(3, 3), dma(3, 3), dma(4, 3), dma(4, 3),
            dma(3), dma(3), dma(4), dma(4),
            dma(3), dma(3),
        ],
        compiler_params=pltpu.CompilerParams(
            collective_id=0, has_side_effects=True, vmem_limit_bytes=60 * 2**20
        ),
        name="extend_add_eliminate",
    )(front.reshape(3, 256, 256), panel_inverse[0], contrib[0], pattern[0].T, front_map[0])
    return out.reshape(1, 768, 256)


def solution(mesh):
    in_specs = (
        P("cube", "row", "col"),
        P("cube", None, None),
        P("cube", ("row", "col"), None, None),
        P("cube", ("row", "col"), None),
        P("cube", None),
    )
    out_specs = P("cube", "row", "col")
    return jax.shard_map(shards, mesh=mesh, in_specs=in_specs, out_specs=out_specs, check_vma=False)
```

```python
import jax
import jax.numpy as jnp
from jax import lax
from jax.experimental import pallas as pl
from jax.experimental.pallas import tpu as pltpu
from jax.sharding import PartitionSpec as P

MESH = pl.DeviceIdType.MESH
PANELS = 4
F32 = jnp.float32
BF16 = jnp.bfloat16
OWN_ROWS = 1024
LEAD_ROWS = 1280
ORDER = (1, 0, 2)


def dot_t(a, b):
    return lax.dot_general(a, b, (((1,), (1,)), ((), ())), preferred_element_type=F32)


def kernel(
    front, winv, contrib, pat, fmap, out,
    cv, fv, wv, sc, cr, own, kept, ys, yr, zs, zr, fx, a_st, l_st, ox, ob,
    lsem, csend, crecv, ysend, yrecv, fsend, frecv, zsend, zrecv,
    gsend, grecv, tsend, trecv, usend, urecv, qsend, qrecv, vsend, vrecv, osend, orecv,
):
    cube = lax.axis_index("cube")
    row = lax.axis_index("row")
    col = lax.axis_index("col")
    cubes = lax.axis_size("cube")
    core = row % 2
    ylo = row // 2
    half = col // 4
    xpos = col % 4

    def at_row_col(r, c):
        return {"row": r, "col": c}

    core_peer = at_row_col(row ^ 1, col)
    y_peers = {m: at_row_col(row ^ (2 * (m & 1)), col ^ (4 * (m >> 1))) for m in (1, 2, 3)}
    x_peers = {m: at_row_col(row, col ^ m) for m in (1, 2, 3)}
    z_peer = {"cube": (cube + cubes // 2) % cubes}

    def remote(src, dst, ssem, rsem, peer):
        return pltpu.make_async_remote_copy(src, dst, ssem, rsem, device_id=peer, device_id_type=MESH)

    barrier = pltpu.get_barrier_semaphore()
    peers = [z_peer, core_peer, *y_peers.values(), *x_peers.values()]
    for p in peers:
        pl.semaphore_signal(barrier, 1, device_id=p, device_id_type=MESH)
    loads = [
        pltpu.make_async_copy(contrib, cv, lsem.at[0]),
        pltpu.make_async_copy(front, fv, lsem.at[1]),
        pltpu.make_async_copy(winv, wv, lsem.at[2]),
    ]
    for c in loads:
        c.start()

    targets = []
    for s in range(6):
        child = pat[0, s]
        targets.append(jnp.where(child >= 0, fmap[jnp.maximum(child, 0)], -1))
    loads[0].wait()

    def c_copy(i):
        return remote(sc.at[i], cr.at[i], csend.at[i], crecv.at[i], core_peer)

    for i in ORDER:
        def masks(y, c):
            block = y * 2 + c + 4 * i
            return [(t == block).astype(F32) for t in targets]

        away = [masks(y, 1 - core) for y in range(2)]
        stay = [masks(y, core) for y in range(2)]

        def tile(t, carry):
            rows = pl.ds(pl.multiple_of(t * 32, 32), 32)
            vals = [cv[s, rows, :].astype(F32) for s in range(6)]

            def total(ms):
                acc = vals[0] * ms[0]
                for v, m in zip(vals[1:], ms[1:]):
                    acc = acc + v * m
                return acc

            for y in range(2):
                sc[i, y, rows, :] = total(away[y]).astype(BF16)
            for y in range(2):
                own[i, y, rows, :] = total(stay[y])
            return carry

        lax.fori_loop(0, 8, tile, 0)

    pl.semaphore_wait(barrier, len(peers))
    for i in ORDER:
        c_copy(i).start()

    own_half = pl.ds(pl.multiple_of(half * 128, 128), 128)
    far_half = pl.ds(pl.multiple_of((1 - half) * 128, 128), 128)

    def y_copy(m, i):
        return remote(ys.at[m - 1, i], yr.at[m - 1, i], ysend.at[m - 1, i], yrecv.at[m - 1, i], y_peers[m])

    def both(i, y, rows):
        return own[i, y, rows, :] + cr[i, y, rows, :].astype(F32)

    for n, i in enumerate(ORDER):
        c_copy(i).wait_recv()
        if n:
            for m in (1, 2, 3):
                y_copy(m, ORDER[n - 1]).wait_send()
        ys[2, i] = both(i, 1 - ylo, far_half).astype(BF16)
        y_copy(3, i).start()
        ys[1, i] = both(i, ylo, far_half).astype(BF16)
        y_copy(2, i).start()
        ys[0, i] = both(i, 1 - ylo, own_half).astype(BF16)
        y_copy(1, i).start()
        kept[i] = both(i, ylo, own_half)

    def z_copy(j, i):
        return remote(zs.at[j, i], zr.at[j, i], zsend.at[j, i], zrecv.at[j, i], z_peer)

    for i in ORDER:
        for m in (1, 2, 3):
            y_copy(m, i).wait_recv()
        zs[half, i] = (kept[i] + yr[0, i].astype(F32)).astype(BF16)
        zs[1 - half, i] = (yr[1, i].astype(F32) + yr[2, i].astype(F32)).astype(BF16)
        z_copy(0, i).start()

    loads[1].wait()
    f_copy = remote(fv.at[:, far_half], fx, fsend, frecv, y_peers[2])
    f_copy.start()

    top = pl.multiple_of(row * 256 + half * 128, 128)

    def rows_of(i):
        return pl.ds(top, 128) if i == 0 else pl.ds(OWN_ROWS + (i - 1) * 128, 128)

    for k in range(PANELS):
        @pl.when(row <= k)
        def _():
            l_st[k, rows_of(0), :] = jnp.zeros((128, 256), BF16)

    f_copy.wait_recv()
    first = half == 0

    def g_copy(m, i):
        ref = a_st.at[xpos, rows_of(i)]
        return remote(ref, ref, gsend.at[m - 1, i], grecv.at[m - 1, i], x_peers[m])

    def g_arrival(m, i):
        ref = a_st.at[xpos ^ m, rows_of(i)]
        return remote(ref, ref, gsend.at[m - 1, i], grecv.at[m - 1, i], x_peers[m])

    def critical(i):
        z_copy(0, i).wait_recv()
        base = jnp.where(first, fv[i, own_half, :].astype(F32), fx[i].astype(F32))
        a_st[xpos, rows_of(i), :] = (base + zr[0, i].astype(F32)).astype(BF16)

    def owner(m):
        return row ^ (2 * (m & 1)), half ^ (m >> 1)

    def tri_place(k, r, h):
        return a_st.at[k, pl.ds(pl.multiple_of(r * 256 + h * 128, 128), 128)]

    def lead_place(h):
        return a_st.at[:, pl.ds(pl.multiple_of(LEAD_ROWS + h * 128, 128), 128)]

    def t_copy(m, k):
        ref = tri_place(k, row, half)
        return remote(ref, ref, tsend.at[m - 1, k], trecv.at[m - 1, k], y_peers[m])

    def t_arrival(m, k):
        ref = tri_place(k, *owner(m))
        return remote(ref, ref, tsend.at[m - 1, k], trecv.at[m - 1, k], y_peers[m])

    def u_copy(m, k):
        ref = tri_place(k, *owner(m))
        return remote(ref, ref, usend.at[m, k], urecv.at[m, k], core_peer)

    def u_arrival(m, k):
        r, h = owner(m)
        ref = tri_place(k, r ^ 1, h)
        return remote(ref, ref, usend.at[m, k], urecv.at[m, k], core_peer)

    def q_copy(m):
        src = a_st.at[:, rows_of(1)]
        return remote(src, lead_place(half), qsend.at[m - 1], qrecv.at[m - 1], y_peers[m])

    def q_arrival(m):
        ref = lead_place(owner(m)[1])
        return remote(ref, ref, qsend.at[m - 1], qrecv.at[m - 1], y_peers[m])

    def v_copy(m):
        ref = lead_place(owner(m)[1])
        src = a_st.at[:, rows_of(1)] if m == 0 else ref
        return remote(src, ref, vsend.at[m], vrecv.at[m], core_peer)

    def each(count, body):
        def step(k, carry):
            body(k)
            return carry

        lax.fori_loop(0, count, step, 0)

    critical(1)
    for m in (1, 2, 3):
        g_copy(m, 1).start()
    z_copy(1, 0).start()

    critical(0)

    @pl.when(row > xpos)
    def _():
        for m in (1, 2, 3):
            g_copy(m, 0).start()

    z_copy(1, 1).start()

    for m in (1, 2, 3):
        g_arrival(m, 1).wait_recv()

    @pl.when(row == xpos)
    def _():
        for m in (3, 1, 2):
            q_copy(m).start()
        v_copy(0).start()
        for k in range(4):
            a_st[k, pl.ds(pl.multiple_of(LEAD_ROWS + half * 128, 128), 128), :] = a_st[k, rows_of(1), :]

    for m in (1, 2, 3):
        @pl.when(row > (xpos ^ m))
        def _():
            g_arrival(m, 0).wait_recv()

    def send_tri(k):
        for m in (3, 1, 2):
            t_copy(m, k).start()
        u_copy(0, k).start()

    each(row, send_tri)

    critical(2)
    for m in (1, 2, 3):
        g_copy(m, 2).start()
    z_copy(1, 2).start()

    for m in (1, 3, 2):
        @pl.when(owner(m)[0] == xpos)
        def _():
            q_arrival(m).wait_recv()
            v_copy(m).start()
    for m in (1, 3, 2):
        def relay_tri(k):
            t_arrival(m, k).wait_recv()
            u_copy(m, k).start()

        each(owner(m)[0], relay_tri)
    for m in range(4):
        each(owner(m)[0] ^ 1, lambda k: u_arrival(m, k).wait_recv())
    loads[2].wait()

    def panel(k, b):
        rows = pl.ds(b * 256, 256)
        acc = a_st[k, rows, :].astype(F32)
        for m in range(k):
            acc = acc - dot_t(l_st[m, rows, :], l_st[m, pl.ds(k * 256, 256), :])
        weight = wv[pl.ds(k * 256, 256), :]
        l_st[k, rows, :] = jnp.dot(acc.astype(BF16), weight, preferred_element_type=F32).astype(BF16)

    for k in range(3):
        for b in range(k + 1, 4):
            panel(k, b)
    for m in (1, 2, 3):
        g_arrival(m, 2).wait_recv()
    for k in range(PANELS):
        panel(k, 4)
    def o_copy(i):
        return remote(ox.at[i], out.at[i, own_half], osend.at[i], orecv.at[i], y_peers[2])

    def keep_copy(i):
        return pltpu.make_async_copy(ob.at[i], out.at[i, own_half], lsem.at[3 + i])

    def o_arrival(i):
        return remote(ox.at[i], out.at[i, far_half], osend.at[i], orecv.at[i], y_peers[2])

    for i in range(3):
        early = l_st[xpos, rows_of(i), :]

        @pl.when(first)
        def _():
            ob[i] = early
            keep_copy(i).start()

        @pl.when(jnp.logical_not(first))
        def _():
            ox[i] = early
            o_copy(i).start()

    for m in range(4):
        @pl.when((owner(m)[0] ^ 1) == xpos)
        def _():
            v_copy(m).wait_recv()

    for k in range(PANELS):
        panel(k, 5)

    for i in range(3):
        acc = jnp.where(first, fx[i].astype(F32), fv[i, own_half, :].astype(F32))
        for k in range(PANELS):
            acc = acc - dot_t(l_st[k, rows_of(i), :], l_st[k, pl.ds(LEAD_ROWS, 256), :])
        z_copy(1, i).wait_recv()
        late = (acc + zr[1, i].astype(F32)).astype(BF16)

        @pl.when(first)
        def _():
            ox[i] = late
            o_copy(i).start()

        @pl.when(jnp.logical_not(first))
        def _():
            ob[i] = late
            keep_copy(i).start()

    for i in range(3):
        o_arrival(i).wait_recv()

    f_copy.wait_send()
    for i in range(3):
        c_copy(i).wait_send()
        o_copy(i).wait_send()
        for m in (1, 2, 3):
            if i == ORDER[-1]:
                y_copy(m, i).wait_send()
            if i:
                g_copy(m, i).wait_send()

    @pl.when(row > xpos)
    def _():
        for m in (1, 2, 3):
            g_copy(m, 0).wait_send()

    def drain_tri(k):
        for m in (1, 2, 3):
            t_copy(m, k).wait_send()

    each(row, drain_tri)
    for m in range(4):
        each(owner(m)[0], lambda k: u_copy(m, k).wait_send())

        @pl.when(owner(m)[0] == xpos)
        def _():
            v_copy(m).wait_send()

    @pl.when(row == xpos)
    def _():
        for m in (1, 2, 3):
            q_copy(m).wait_send()

    for i in range(3):
        for j in range(2):
            z_copy(j, i).wait_send()
    for i in range(3):
        keep_copy(i).wait()


def shards(front, panel_inverse, contrib, pattern, front_map):
    hbm = pl.BlockSpec(memory_space=pl.ANY)
    smem = pl.BlockSpec(memory_space=pltpu.SMEM)

    def vmem(*shape, dtype=BF16):
        return pltpu.VMEM(shape, dtype)

    def dma(*shape):
        return pltpu.SemaphoreType.DMA(shape)

    out = pl.pallas_call(
        kernel,
        out_shape=jax.ShapeDtypeStruct((3, 256, 256), BF16),
        in_specs=[hbm, hbm, hbm, smem, smem],
        out_specs=hbm,
        scratch_shapes=[
            vmem(6, 256, 256),
            vmem(3, 256, 256),
            vmem(1024, 256),
            vmem(3, 2, 256, 256),
            vmem(3, 2, 256, 256),
            vmem(3, 2, 256, 256, dtype=F32),
            vmem(3, 128, 256, dtype=F32),
            vmem(3, 3, 128, 256),
            vmem(3, 3, 128, 256),
            vmem(2, 3, 128, 256),
            vmem(2, 3, 128, 256),
            vmem(3, 128, 256),
            vmem(4, 1536, 256),
            vmem(4, 1536, 256),
            vmem(3, 128, 256),
            vmem(3, 128, 256),
            dma(6),
            dma(3), dma(3), dma(3, 3), dma(3, 3),
            pltpu.SemaphoreType.DMA, pltpu.SemaphoreType.DMA,
            dma(2, 3), dma(2, 3),
            dma(3, 3), dma(3, 3),
            dma(3, 3), dma(3, 3), dma(4, 3), dma(4, 3),
            dma(3), dma(3), dma(4), dma(4),
            dma(3), dma(3),
        ],
        compiler_params=pltpu.CompilerParams(
            collective_id=0, has_side_effects=True, vmem_limit_bytes=60 * 2**20
        ),
        name="extend_add_eliminate",
    )(front.reshape(3, 256, 256), panel_inverse[0], contrib[0], pattern[0].T, front_map[0])
    return out.reshape(1, 768, 256)


def solution(mesh):
    in_specs = (
        P("cube", "row", "col"),
        P("cube", None, None),
        P("cube", ("row", "col"), None, None),
        P("cube", ("row", "col"), None),
        P("cube", None),
    )
    out_specs = P("cube", "row", "col")
    return jax.shard_map(shards, mesh=mesh, in_specs=in_specs, out_specs=out_specs, check_vma=False)
```

```python
import jax
import jax.numpy as jnp
from jax import lax
from jax.experimental import pallas as pl
from jax.experimental.pallas import tpu as pltpu
from jax.sharding import PartitionSpec as P

MESH = pl.DeviceIdType.MESH
PANELS = 4
F32 = jnp.float32
BF16 = jnp.bfloat16
OWN_ROWS = 1024
LEAD_ROWS = 1280
ORDER = (1, 0, 2)


def dot_t(a, b):
    return lax.dot_general(a, b, (((1,), (1,)), ((), ())), preferred_element_type=F32)


def kernel(
    front, winv, contrib, pat, fmap, out,
    cv, fv, wv, sc, cr, own, kept, ys, yr, zs, zr, fx, a_st, l_st, ox, ob,
    lsem, csend, crecv, ysend, yrecv, fsend, frecv, zsend, zrecv,
    gsend, grecv, tsend, trecv, usend, urecv, qsend, qrecv, vsend, vrecv, osend, orecv,
):
    cube = lax.axis_index("cube")
    row = lax.axis_index("row")
    col = lax.axis_index("col")
    cubes = lax.axis_size("cube")
    core = row % 2
    ylo = row // 2
    half = col // 4
    xpos = col % 4

    def at_row_col(r, c):
        return {"row": r, "col": c}

    core_peer = at_row_col(row ^ 1, col)
    y_peers = {m: at_row_col(row ^ (2 * (m & 1)), col ^ (4 * (m >> 1))) for m in (1, 2, 3)}
    x_peers = {m: at_row_col(row, col ^ m) for m in (1, 2, 3)}
    z_peer = {"cube": (cube + cubes // 2) % cubes}

    def remote(src, dst, ssem, rsem, peer):
        return pltpu.make_async_remote_copy(src, dst, ssem, rsem, device_id=peer, device_id_type=MESH)

    barrier = pltpu.get_barrier_semaphore()
    peers = [z_peer, core_peer, *y_peers.values(), *x_peers.values()]
    for p in peers:
        pl.semaphore_signal(barrier, 1, device_id=p, device_id_type=MESH)
    loads = [
        pltpu.make_async_copy(contrib, cv, lsem.at[0]),
        pltpu.make_async_copy(front, fv, lsem.at[1]),
        pltpu.make_async_copy(winv, wv, lsem.at[2]),
    ]
    loads[0].start()

    targets = []
    for s in range(6):
        child = pat[0, s]
        targets.append(jnp.where(child >= 0, fmap[jnp.maximum(child, 0)], -1))
    loads[0].wait()
    loads[1].start()
    loads[2].start()

    def c_copy(i):
        return remote(sc.at[i], cr.at[i], csend.at[i], crecv.at[i], core_peer)

    def totals(i, c, put):
        masks = [[(t == y * 2 + c + 4 * i).astype(F32) for t in targets] for y in range(2)]

        def tile(t, carry):
            rows = pl.ds(pl.multiple_of(t * 32, 32), 32)
            vals = [cv[s, rows, :].astype(F32) for s in range(6)]
            for y in range(2):
                acc = vals[0] * masks[y][0]
                for v, m in zip(vals[1:], masks[y][1:]):
                    acc = acc + v * m
                put(y, rows, acc)
            return carry

        lax.fori_loop(0, 8, tile, 0)

    def put_away(i):
        def put(y, rows, acc):
            sc[i, y, rows, :] = acc.astype(BF16)

        return put

    def put_own(i):
        def put(y, rows, acc):
            own[i, y, rows, :] = acc

        return put

    for i in ORDER:
        totals(i, 1 - core, put_away(i))
        if i == ORDER[0]:
            pl.semaphore_wait(barrier, len(peers))
        c_copy(i).start()
        totals(i, core, put_own(i))

    own_half = pl.ds(pl.multiple_of(half * 128, 128), 128)
    far_half = pl.ds(pl.multiple_of((1 - half) * 128, 128), 128)

    def y_copy(m, i):
        return remote(ys.at[m - 1, i], yr.at[m - 1, i], ysend.at[m - 1, i], yrecv.at[m - 1, i], y_peers[m])

    def both(i, y, rows):
        return own[i, y, rows, :] + cr[i, y, rows, :].astype(F32)

    for i in ORDER:
        c_copy(i).wait_recv()
        ys[2, i] = both(i, 1 - ylo, far_half).astype(BF16)
        y_copy(3, i).start()
        ys[1, i] = both(i, ylo, far_half).astype(BF16)
        y_copy(2, i).start()
        ys[0, i] = both(i, 1 - ylo, own_half).astype(BF16)
        y_copy(1, i).start()
        kept[i] = both(i, ylo, own_half)

    def z_copy(j, i):
        return remote(zs.at[j, i], zr.at[j, i], zsend.at[j, i], zrecv.at[j, i], z_peer)

    first = half == 0

    def near_sum(j, i):
        y_copy(1, i).wait_recv()
        zs[j, i] = (kept[i] + yr[0, i].astype(F32)).astype(BF16)

    def far_sum(j, i):
        y_copy(2, i).wait_recv()
        y_copy(3, i).wait_recv()
        zs[j, i] = (yr[1, i].astype(F32) + yr[2, i].astype(F32)).astype(BF16)

    for i in ORDER:
        @pl.when(first)
        def _():
            near_sum(0, i)

        @pl.when(jnp.logical_not(first))
        def _():
            far_sum(0, i)

        z_copy(0, i).start()

    for i in range(3):
        @pl.when(first)
        def _():
            far_sum(1, i)

        @pl.when(jnp.logical_not(first))
        def _():
            near_sum(1, i)

    loads[1].wait()
    f_copy = remote(fv.at[:, far_half], fx, fsend, frecv, y_peers[2])
    f_copy.start()

    top = pl.multiple_of(row * 256 + half * 128, 128)

    def rows_of(i):
        return pl.ds(top, 128) if i == 0 else pl.ds(OWN_ROWS + (i - 1) * 128, 128)

    for k in range(PANELS):
        @pl.when(row <= k)
        def _():
            l_st[k, rows_of(0), :] = jnp.zeros((128, 256), BF16)

    f_copy.wait_recv()

    def g_copy(m, i):
        ref = a_st.at[xpos, rows_of(i)]
        return remote(ref, ref, gsend.at[m - 1, i], grecv.at[m - 1, i], x_peers[m])

    def g_arrival(m, i):
        ref = a_st.at[xpos ^ m, rows_of(i)]
        return remote(ref, ref, gsend.at[m - 1, i], grecv.at[m - 1, i], x_peers[m])

    def critical(i):
        z_copy(0, i).wait_recv()
        base = jnp.where(first, fv[i, own_half, :].astype(F32), fx[i].astype(F32))
        a_st[xpos, rows_of(i), :] = (base + zr[0, i].astype(F32)).astype(BF16)

    def owner(m):
        return row ^ (2 * (m & 1)), half ^ (m >> 1)

    def tri_place(k, r, h):
        return a_st.at[k, pl.ds(pl.multiple_of(r * 256 + h * 128, 128), 128)]

    def lead_place(k, h):
        return a_st.at[k, pl.ds(pl.multiple_of(LEAD_ROWS + h * 128, 128), 128)]

    def t_copy(m, k):
        ref = tri_place(k, row, half)
        return remote(ref, ref, tsend.at[m - 1, k], trecv.at[m - 1, k], y_peers[m])

    def t_arrival(m, k):
        ref = tri_place(k, *owner(m))
        return remote(ref, ref, tsend.at[m - 1, k], trecv.at[m - 1, k], y_peers[m])

    def u_copy(m, k):
        ref = tri_place(k, *owner(m))
        return remote(ref, ref, usend.at[m, k], urecv.at[m, k], core_peer)

    def u_arrival(m, k):
        r, h = owner(m)
        ref = tri_place(k, r ^ 1, h)
        return remote(ref, ref, usend.at[m, k], urecv.at[m, k], core_peer)

    def q_copy(m, k):
        src = a_st.at[k, rows_of(1)]
        return remote(src, lead_place(k, half), qsend.at[m - 1, k], qrecv.at[m - 1, k], y_peers[m])

    def q_arrival(m, k):
        ref = lead_place(k, owner(m)[1])
        return remote(ref, ref, qsend.at[m - 1, k], qrecv.at[m - 1, k], y_peers[m])

    def v_copy(m, k):
        ref = lead_place(k, owner(m)[1])
        src = a_st.at[k, rows_of(1)] if m == 0 else ref
        return remote(src, ref, vsend.at[m, k], vrecv.at[m, k], core_peer)

    def each(count, body):
        def step(k, carry):
            body(k)
            return carry

        lax.fori_loop(0, count, step, 0)

    def send_lead(k):
        @pl.when(row == xpos)
        def _():
            for m in (3, 1, 2):
                q_copy(m, k).start()
            v_copy(0, k).start()

    def send_tri(k):
        @pl.when(row > k)
        def _():
            for m in (3, 1, 2):
                t_copy(m, k).start()
            u_copy(0, k).start()

    critical(1)
    for m in (1, 3, 2):
        g_copy(m, 1).start()
    send_lead(xpos)
    z_copy(1, 0).start()

    critical(0)

    @pl.when(row > xpos)
    def _():
        for m in (1, 3, 2):
            g_copy(m, 0).start()

    send_tri(xpos)
    z_copy(1, 1).start()

    for m in (1, 3, 2):
        g_arrival(m, 1).wait_recv()
        send_lead(xpos ^ m)

        @pl.when(row > (xpos ^ m))
        def _():
            g_arrival(m, 0).wait_recv()

        send_tri(xpos ^ m)

    @pl.when(row == xpos)
    def _():
        for k in range(4):
            a_st[k, pl.ds(pl.multiple_of(LEAD_ROWS + half * 128, 128), 128), :] = a_st[k, rows_of(1), :]

    critical(2)
    for m in (1, 3, 2):
        g_copy(m, 2).start()
    z_copy(1, 2).start()

    for n in (0, 1, 3, 2):
        k = xpos ^ n
        for m in (1, 3, 2):
            @pl.when(owner(m)[0] == xpos)
            def _():
                q_arrival(m, k).wait_recv()
                v_copy(m, k).start()

            @pl.when(owner(m)[0] > k)
            def _():
                t_arrival(m, k).wait_recv()
                u_copy(m, k).start()

    for m in range(4):
        each(owner(m)[0] ^ 1, lambda k: u_arrival(m, k).wait_recv())
    loads[2].wait()

    def panel(k, b):
        rows = pl.ds(b * 256, 256)
        acc = a_st[k, rows, :].astype(F32)
        for m in range(k):
            acc = acc - dot_t(l_st[m, rows, :], l_st[m, pl.ds(k * 256, 256), :])
        weight = wv[pl.ds(k * 256, 256), :]
        l_st[k, rows, :] = jnp.dot(acc.astype(BF16), weight, preferred_element_type=F32).astype(BF16)

    for k in range(3):
        for b in range(k + 1, 4):
            panel(k, b)
    for m in (1, 2, 3):
        g_arrival(m, 2).wait_recv()
    for k in range(PANELS):
        panel(k, 4)
    def o_copy(i):
        return remote(ox.at[i], out.at[i, own_half], osend.at[i], orecv.at[i], y_peers[2])

    def keep_copy(i):
        return pltpu.make_async_copy(ob.at[i], out.at[i, own_half], lsem.at[3 + i])

    def o_arrival(i):
        return remote(ox.at[i], out.at[i, far_half], osend.at[i], orecv.at[i], y_peers[2])

    for i in range(3):
        early = l_st[xpos, rows_of(i), :]

        @pl.when(first)
        def _():
            ob[i] = early
            keep_copy(i).start()

        @pl.when(jnp.logical_not(first))
        def _():
            ox[i] = early
            o_copy(i).start()

    for m in range(4):
        @pl.when((owner(m)[0] ^ 1) == xpos)
        def _():
            for k in range(4):
                v_copy(m, k).wait_recv()

    for k in range(PANELS):
        panel(k, 5)

    for i in range(3):
        acc = jnp.where(first, fx[i].astype(F32), fv[i, own_half, :].astype(F32))
        for k in range(PANELS):
            acc = acc - dot_t(l_st[k, rows_of(i), :], l_st[k, pl.ds(LEAD_ROWS, 256), :])
        z_copy(1, i).wait_recv()
        late = (acc + zr[1, i].astype(F32)).astype(BF16)

        @pl.when(first)
        def _():
            ox[i] = late
            o_copy(i).start()

        @pl.when(jnp.logical_not(first))
        def _():
            ob[i] = late
            keep_copy(i).start()

    for i in range(3):
        o_arrival(i).wait_recv()

    f_copy.wait_send()
    for i in range(3):
        c_copy(i).wait_send()
        o_copy(i).wait_send()
        for m in (1, 2, 3):
            y_copy(m, i).wait_send()
            if i:
                g_copy(m, i).wait_send()

    @pl.when(row > xpos)
    def _():
        for m in (1, 2, 3):
            g_copy(m, 0).wait_send()

    def drain_tri(k):
        for m in (1, 2, 3):
            t_copy(m, k).wait_send()

    each(row, drain_tri)
    for m in range(4):
        each(owner(m)[0], lambda k: u_copy(m, k).wait_send())

        @pl.when(owner(m)[0] == xpos)
        def _():
            for k in range(4):
                v_copy(m, k).wait_send()

    @pl.when(row == xpos)
    def _():
        for m in (1, 2, 3):
            for k in range(4):
                q_copy(m, k).wait_send()

    for i in range(3):
        for j in range(2):
            z_copy(j, i).wait_send()
    for i in range(3):
        keep_copy(i).wait()


def shards(front, panel_inverse, contrib, pattern, front_map):
    hbm = pl.BlockSpec(memory_space=pl.ANY)
    smem = pl.BlockSpec(memory_space=pltpu.SMEM)

    def vmem(*shape, dtype=BF16):
        return pltpu.VMEM(shape, dtype)

    def dma(*shape):
        return pltpu.SemaphoreType.DMA(shape)

    out = pl.pallas_call(
        kernel,
        out_shape=jax.ShapeDtypeStruct((3, 256, 256), BF16),
        in_specs=[hbm, hbm, hbm, smem, smem],
        out_specs=hbm,
        scratch_shapes=[
            vmem(6, 256, 256),
            vmem(3, 256, 256),
            vmem(1024, 256),
            vmem(3, 2, 256, 256),
            vmem(3, 2, 256, 256),
            vmem(3, 2, 256, 256, dtype=F32),
            vmem(3, 128, 256, dtype=F32),
            vmem(3, 3, 128, 256),
            vmem(3, 3, 128, 256),
            vmem(2, 3, 128, 256),
            vmem(2, 3, 128, 256),
            vmem(3, 128, 256),
            vmem(4, 1536, 256),
            vmem(4, 1536, 256),
            vmem(3, 128, 256),
            vmem(3, 128, 256),
            dma(6),
            dma(3), dma(3), dma(3, 3), dma(3, 3),
            pltpu.SemaphoreType.DMA, pltpu.SemaphoreType.DMA,
            dma(2, 3), dma(2, 3),
            dma(3, 3), dma(3, 3),
            dma(3, 3), dma(3, 3), dma(4, 3), dma(4, 3),
            dma(3, 4), dma(3, 4), dma(4, 4), dma(4, 4),
            dma(3), dma(3),
        ],
        compiler_params=pltpu.CompilerParams(
            collective_id=0, has_side_effects=True, vmem_limit_bytes=107 * 2**19
        ),
        name="extend_add_eliminate",
    )(front.reshape(3, 256, 256), panel_inverse[0], contrib[0], pattern[0].T, front_map[0])
    return out.reshape(1, 768, 256)


def solution(mesh):
    in_specs = (
        P("cube", "row", "col"),
        P("cube", None, None),
        P("cube", ("row", "col"), None, None),
        P("cube", ("row", "col"), None),
        P("cube", None),
    )
    out_specs = P("cube", "row", "col")
    return jax.shard_map(shards, mesh=mesh, in_specs=in_specs, out_specs=out_specs, check_vma=False)
```

```python
import jax
import jax.numpy as jnp
from jax import lax
from jax.experimental import pallas as pl
from jax.experimental.pallas import tpu as pltpu
from jax.sharding import PartitionSpec as P

MESH = pl.DeviceIdType.MESH
PANELS = 4
F32 = jnp.float32
BF16 = jnp.bfloat16
OWN_ROWS = 1024
LEAD_ROWS = 1280
ORDER = (1, 0, 2)


def dot_t(a, b):
    return lax.dot_general(a, b, (((1,), (1,)), ((), ())), preferred_element_type=F32)


def kernel(
    front, winv, contrib, pat, fmap, out,
    cv, fv, wv, sc, cr, own, kept, ys, yr, zs, zr, fx, a_st, l_st, ox, ob,
    lsem, csend, crecv, ysend, yrecv, fsend, frecv, zsend, zrecv,
    gsend, grecv, tsend, trecv, usend, urecv, qsend, qrecv, vsend, vrecv, osend, orecv,
):
    cube = lax.axis_index("cube")
    row = lax.axis_index("row")
    col = lax.axis_index("col")
    cubes = lax.axis_size("cube")
    core = row % 2
    ylo = row // 2
    half = col // 4
    xpos = col % 4

    def at_row_col(r, c):
        return {"row": r, "col": c}

    core_peer = at_row_col(row ^ 1, col)
    y_peers = {m: at_row_col(row ^ (2 * (m & 1)), col ^ (4 * (m >> 1))) for m in (1, 2, 3)}
    x_peers = {m: at_row_col(row, col ^ m) for m in (1, 2, 3)}
    z_peer = {"cube": (cube + cubes // 2) % cubes}

    def remote(src, dst, ssem, rsem, peer):
        return pltpu.make_async_remote_copy(src, dst, ssem, rsem, device_id=peer, device_id_type=MESH)

    barrier = pltpu.get_barrier_semaphore()
    peers = [z_peer, core_peer, *y_peers.values(), *x_peers.values()]
    for p in peers:
        pl.semaphore_signal(barrier, 1, device_id=p, device_id_type=MESH)
    loads = [
        pltpu.make_async_copy(contrib, cv, lsem.at[0]),
        pltpu.make_async_copy(front, fv, lsem.at[1]),
        pltpu.make_async_copy(winv, wv, lsem.at[2]),
    ]
    loads[0].start()

    targets = []
    for s in range(6):
        child = pat[0, s]
        targets.append(jnp.where(child >= 0, fmap[jnp.maximum(child, 0)], -1))
    loads[0].wait()
    loads[1].start()
    loads[2].start()

    def c_copy(i):
        return remote(sc.at[i], cr.at[i], csend.at[i], crecv.at[i], core_peer)

    def totals(i, c, put):
        masks = [[(t == y * 2 + c + 4 * i).astype(F32) for t in targets] for y in range(2)]

        def tile(t, carry):
            rows = pl.ds(pl.multiple_of(t * 16, 16), 16)
            vals = [cv[s, rows, :].astype(F32) for s in range(6)]
            for y in range(2):
                acc = vals[0] * masks[y][0]
                for v, m in zip(vals[1:], masks[y][1:]):
                    acc = acc + v * m
                put(y, rows, acc)
            return carry

        lax.fori_loop(0, 16, tile, 0, unroll=4)

    def put_away(i):
        def put(y, rows, acc):
            sc[i, y, rows, :] = acc.astype(BF16)

        return put

    def put_own(i):
        def put(y, rows, acc):
            own[i, y, rows, :] = acc

        return put

    for i in ORDER:
        totals(i, 1 - core, put_away(i))
        if i == ORDER[0]:
            pl.semaphore_wait(barrier, len(peers))
        c_copy(i).start()
        totals(i, core, put_own(i))

    own_half = pl.ds(pl.multiple_of(half * 128, 128), 128)
    far_half = pl.ds(pl.multiple_of((1 - half) * 128, 128), 128)

    def y_copy(m, i):
        return remote(ys.at[m - 1, i], yr.at[m - 1, i], ysend.at[m - 1, i], yrecv.at[m - 1, i], y_peers[m])

    def both(i, y, rows):
        return own[i, y, rows, :] + cr[i, y, rows, :].astype(F32)

    for i in ORDER:
        c_copy(i).wait_recv()
        ys[2, i] = both(i, 1 - ylo, far_half).astype(BF16)
        y_copy(3, i).start()
        ys[1, i] = both(i, ylo, far_half).astype(BF16)
        y_copy(2, i).start()
        ys[0, i] = both(i, 1 - ylo, own_half).astype(BF16)
        y_copy(1, i).start()
        kept[i] = both(i, ylo, own_half)

    def z_copy(j, i):
        return remote(zs.at[j, i], zr.at[j, i], zsend.at[j, i], zrecv.at[j, i], z_peer)

    first = half == 0

    def near_sum(j, i):
        y_copy(1, i).wait_recv()
        zs[j, i] = (kept[i] + yr[0, i].astype(F32)).astype(BF16)

    def far_sum(j, i):
        y_copy(2, i).wait_recv()
        y_copy(3, i).wait_recv()
        zs[j, i] = (yr[1, i].astype(F32) + yr[2, i].astype(F32)).astype(BF16)

    for i in ORDER:
        @pl.when(first)
        def _():
            near_sum(0, i)

        @pl.when(jnp.logical_not(first))
        def _():
            far_sum(0, i)

        z_copy(0, i).start()

    for i in range(3):
        @pl.when(first)
        def _():
            far_sum(1, i)

        @pl.when(jnp.logical_not(first))
        def _():
            near_sum(1, i)

    loads[1].wait()
    f_copy = remote(fv.at[:, far_half], fx, fsend, frecv, y_peers[2])
    f_copy.start()

    top = pl.multiple_of(row * 256 + half * 128, 128)

    def rows_of(i):
        return pl.ds(top, 128) if i == 0 else pl.ds(OWN_ROWS + (i - 1) * 128, 128)

    for k in range(PANELS):
        @pl.when(row <= k)
        def _():
            l_st[k, rows_of(0), :] = jnp.zeros((128, 256), BF16)

    f_copy.wait_recv()

    def g_copy(m, i):
        ref = a_st.at[xpos, rows_of(i)]
        return remote(ref, ref, gsend.at[m - 1, i], grecv.at[m - 1, i], x_peers[m])

    def g_arrival(m, i):
        ref = a_st.at[xpos ^ m, rows_of(i)]
        return remote(ref, ref, gsend.at[m - 1, i], grecv.at[m - 1, i], x_peers[m])

    def critical(i):
        z_copy(0, i).wait_recv()
        base = jnp.where(first, fv[i, own_half, :].astype(F32), fx[i].astype(F32))
        a_st[xpos, rows_of(i), :] = (base + zr[0, i].astype(F32)).astype(BF16)

    def owner(m):
        return row ^ (2 * (m & 1)), half ^ (m >> 1)

    def tri_place(k, r, h):
        return a_st.at[k, pl.ds(pl.multiple_of(r * 256 + h * 128, 128), 128)]

    def lead_place(k, h):
        return a_st.at[k, pl.ds(pl.multiple_of(LEAD_ROWS + h * 128, 128), 128)]

    def t_copy(m, k):
        ref = tri_place(k, row, half)
        return remote(ref, ref, tsend.at[m - 1, k], trecv.at[m - 1, k], y_peers[m])

    def t_arrival(m, k):
        ref = tri_place(k, *owner(m))
        return remote(ref, ref, tsend.at[m - 1, k], trecv.at[m - 1, k], y_peers[m])

    def u_copy(m, k):
        ref = tri_place(k, *owner(m))
        return remote(ref, ref, usend.at[m, k], urecv.at[m, k], core_peer)

    def u_arrival(m, k):
        r, h = owner(m)
        ref = tri_place(k, r ^ 1, h)
        return remote(ref, ref, usend.at[m, k], urecv.at[m, k], core_peer)

    def q_copy(m, k):
        src = a_st.at[k, rows_of(1)]
        return remote(src, lead_place(k, half), qsend.at[m - 1, k], qrecv.at[m - 1, k], y_peers[m])

    def q_arrival(m, k):
        ref = lead_place(k, owner(m)[1])
        return remote(ref, ref, qsend.at[m - 1, k], qrecv.at[m - 1, k], y_peers[m])

    def v_copy(m, k):
        ref = lead_place(k, owner(m)[1])
        src = a_st.at[k, rows_of(1)] if m == 0 else ref
        return remote(src, ref, vsend.at[m, k], vrecv.at[m, k], core_peer)

    def each(count, body):
        def step(k, carry):
            body(k)
            return carry

        lax.fori_loop(0, count, step, 0)

    def send_lead(k):
        @pl.when(row == xpos)
        def _():
            for m in (3, 1, 2):
                q_copy(m, k).start()
            v_copy(0, k).start()

    def send_tri(k):
        @pl.when(row > k)
        def _():
            for m in (3, 1, 2):
                t_copy(m, k).start()
            u_copy(0, k).start()

    critical(1)
    for m in (1, 3, 2):
        g_copy(m, 1).start()
    send_lead(xpos)
    z_copy(1, 0).start()

    critical(0)

    @pl.when(row > xpos)
    def _():
        for m in (1, 3, 2):
            g_copy(m, 0).start()

    send_tri(xpos)
    z_copy(1, 1).start()

    for m in (1, 3, 2):
        g_arrival(m, 1).wait_recv()
        send_lead(xpos ^ m)

        @pl.when(row > (xpos ^ m))
        def _():
            g_arrival(m, 0).wait_recv()

        send_tri(xpos ^ m)

    @pl.when(row == xpos)
    def _():
        for k in range(4):
            a_st[k, pl.ds(pl.multiple_of(LEAD_ROWS + half * 128, 128), 128), :] = a_st[k, rows_of(1), :]

    critical(2)
    for m in (1, 3, 2):
        g_copy(m, 2).start()
    z_copy(1, 2).start()

    for n in (0, 1, 3, 2):
        k = xpos ^ n
        for m in (1, 3, 2):
            @pl.when(owner(m)[0] == xpos)
            def _():
                q_arrival(m, k).wait_recv()
                v_copy(m, k).start()

            @pl.when(owner(m)[0] > k)
            def _():
                t_arrival(m, k).wait_recv()
                u_copy(m, k).start()

    for m in range(4):
        each(owner(m)[0] ^ 1, lambda k: u_arrival(m, k).wait_recv())
    loads[2].wait()

    def panel(k, b):
        rows = pl.ds(b * 256, 256)
        acc = a_st[k, rows, :].astype(F32)
        for m in range(k):
            acc = acc - dot_t(l_st[m, rows, :], l_st[m, pl.ds(k * 256, 256), :])
        weight = wv[pl.ds(k * 256, 256), :]
        l_st[k, rows, :] = jnp.dot(acc.astype(BF16), weight, preferred_element_type=F32).astype(BF16)

    for k in range(3):
        for b in range(k + 1, 4):
            panel(k, b)
    for m in (1, 2, 3):
        g_arrival(m, 2).wait_recv()
    for k in range(PANELS):
        panel(k, 4)
    def o_copy(i):
        return remote(ox.at[i], out.at[i, own_half], osend.at[i], orecv.at[i], y_peers[2])

    def keep_copy(i):
        return pltpu.make_async_copy(ob.at[i], out.at[i, own_half], lsem.at[3 + i])

    def o_arrival(i):
        return remote(ox.at[i], out.at[i, far_half], osend.at[i], orecv.at[i], y_peers[2])

    for i in range(3):
        early = l_st[xpos, rows_of(i), :]

        @pl.when(first)
        def _():
            ob[i] = early
            keep_copy(i).start()

        @pl.when(jnp.logical_not(first))
        def _():
            ox[i] = early
            o_copy(i).start()

    for m in range(4):
        @pl.when((owner(m)[0] ^ 1) == xpos)
        def _():
            for k in range(4):
                v_copy(m, k).wait_recv()

    for k in range(PANELS):
        panel(k, 5)

    for i in range(3):
        acc = jnp.where(first, fx[i].astype(F32), fv[i, own_half, :].astype(F32))
        for k in range(PANELS):
            acc = acc - dot_t(l_st[k, rows_of(i), :], l_st[k, pl.ds(LEAD_ROWS, 256), :])
        z_copy(1, i).wait_recv()
        late = (acc + zr[1, i].astype(F32)).astype(BF16)

        @pl.when(first)
        def _():
            ox[i] = late
            o_copy(i).start()

        @pl.when(jnp.logical_not(first))
        def _():
            ob[i] = late
            keep_copy(i).start()

    for i in range(3):
        o_arrival(i).wait_recv()

    f_copy.wait_send()
    for i in range(3):
        c_copy(i).wait_send()
        o_copy(i).wait_send()
        for m in (1, 2, 3):
            y_copy(m, i).wait_send()
            if i:
                g_copy(m, i).wait_send()

    @pl.when(row > xpos)
    def _():
        for m in (1, 2, 3):
            g_copy(m, 0).wait_send()

    def drain_tri(k):
        for m in (1, 2, 3):
            t_copy(m, k).wait_send()

    each(row, drain_tri)
    for m in range(4):
        each(owner(m)[0], lambda k: u_copy(m, k).wait_send())

        @pl.when(owner(m)[0] == xpos)
        def _():
            for k in range(4):
                v_copy(m, k).wait_send()

    @pl.when(row == xpos)
    def _():
        for m in (1, 2, 3):
            for k in range(4):
                q_copy(m, k).wait_send()

    for i in range(3):
        for j in range(2):
            z_copy(j, i).wait_send()
    for i in range(3):
        keep_copy(i).wait()


def shards(front, panel_inverse, contrib, pattern, front_map):
    hbm = pl.BlockSpec(memory_space=pl.ANY)
    smem = pl.BlockSpec(memory_space=pltpu.SMEM)

    def vmem(*shape, dtype=BF16):
        return pltpu.VMEM(shape, dtype)

    def dma(*shape):
        return pltpu.SemaphoreType.DMA(shape)

    out = pl.pallas_call(
        kernel,
        out_shape=jax.ShapeDtypeStruct((3, 256, 256), BF16),
        in_specs=[hbm, hbm, hbm, smem, smem],
        out_specs=hbm,
        scratch_shapes=[
            vmem(6, 256, 256),
            vmem(3, 256, 256),
            vmem(1024, 256),
            vmem(3, 2, 256, 256),
            vmem(3, 2, 256, 256),
            vmem(3, 2, 256, 256, dtype=F32),
            vmem(3, 128, 256, dtype=F32),
            vmem(3, 3, 128, 256),
            vmem(3, 3, 128, 256),
            vmem(2, 3, 128, 256),
            vmem(2, 3, 128, 256),
            vmem(3, 128, 256),
            vmem(4, 1536, 256),
            vmem(4, 1536, 256),
            vmem(3, 128, 256),
            vmem(3, 128, 256),
            dma(6),
            dma(3), dma(3), dma(3, 3), dma(3, 3),
            pltpu.SemaphoreType.DMA, pltpu.SemaphoreType.DMA,
            dma(2, 3), dma(2, 3),
            dma(3, 3), dma(3, 3),
            dma(3, 3), dma(3, 3), dma(4, 3), dma(4, 3),
            dma(3, 4), dma(3, 4), dma(4, 4), dma(4, 4),
            dma(3), dma(3),
        ],
        compiler_params=pltpu.CompilerParams(
            collective_id=0, has_side_effects=True, vmem_limit_bytes=107 * 2**19
        ),
        name="extend_add_eliminate",
    )(front.reshape(3, 256, 256), panel_inverse[0], contrib[0], pattern[0].T, front_map[0])
    return out.reshape(1, 768, 256)


def solution(mesh):
    in_specs = (
        P("cube", "row", "col"),
        P("cube", None, None),
        P("cube", ("row", "col"), None, None),
        P("cube", ("row", "col"), None),
        P("cube", None),
    )
    out_specs = P("cube", "row", "col")
    return jax.shard_map(shards, mesh=mesh, in_specs=in_specs, out_specs=out_specs, check_vma=False)
```

```python
import jax
import jax.numpy as jnp
from jax import lax
from jax.experimental import pallas as pl
from jax.experimental.pallas import tpu as pltpu
from jax.sharding import PartitionSpec as P

MESH = pl.DeviceIdType.MESH
PANELS = 4
F32 = jnp.float32
BF16 = jnp.bfloat16
OWN_ROWS = 1024
LEAD_ROWS = 1280
ORDER = (1, 0, 2)


def dot_t(a, b):
    return lax.dot_general(a, b, (((1,), (1,)), ((), ())), preferred_element_type=F32)


def kernel(
    front, winv, contrib, pat, fmap, out,
    cv, fv, wv, sc, cr, own, kept, ys, yr, zs, zr, fx, a_st, l_st, ox, ob,
    lsem, csend, crecv, ysend, yrecv, fsend, frecv, zsend, zrecv,
    gsend, grecv, tsend, trecv, usend, urecv, qsend, qrecv, vsend, vrecv, osend, orecv,
):
    cube = lax.axis_index("cube")
    row = lax.axis_index("row")
    col = lax.axis_index("col")
    cubes = lax.axis_size("cube")
    core = row % 2
    ylo = row // 2
    half = col // 4
    xpos = col % 4

    def at_row_col(r, c):
        return {"row": r, "col": c}

    core_peer = at_row_col(row ^ 1, col)
    y_peers = {m: at_row_col(row ^ (2 * (m & 1)), col ^ (4 * (m >> 1))) for m in (1, 2, 3)}
    x_peers = {m: at_row_col(row, col ^ m) for m in (1, 2, 3)}
    z_peer = {"cube": (cube + cubes // 2) % cubes}

    def remote(src, dst, ssem, rsem, peer):
        return pltpu.make_async_remote_copy(src, dst, ssem, rsem, device_id=peer, device_id_type=MESH)

    barrier = pltpu.get_barrier_semaphore()
    peers = [z_peer, core_peer, *y_peers.values(), *x_peers.values()]
    for p in peers:
        pl.semaphore_signal(barrier, 1, device_id=p, device_id_type=MESH)
    loads = [
        pltpu.make_async_copy(contrib, cv, lsem.at[0]),
        pltpu.make_async_copy(front, fv, lsem.at[1]),
        pltpu.make_async_copy(winv, wv, lsem.at[2]),
    ]
    loads[0].start()

    targets = []
    for s in range(6):
        child = pat[0, s]
        targets.append(jnp.where(child >= 0, fmap[jnp.maximum(child, 0)], -1))
    loads[0].wait()
    loads[1].start()
    loads[2].start()

    def c_copy(i):
        return remote(sc.at[i], cr.at[i], csend.at[i], crecv.at[i], core_peer)

    def totals(i, c, put):
        masks = [[(t == y * 2 + c + 4 * i).astype(F32) for t in targets] for y in range(2)]

        def tile(t, carry):
            rows = pl.ds(pl.multiple_of(t * 16, 16), 16)
            vals = [cv[s, rows, :].astype(F32) for s in range(6)]
            for y in range(2):
                acc = vals[0] * masks[y][0]
                for v, m in zip(vals[1:], masks[y][1:]):
                    acc = acc + v * m
                put(y, rows, acc)
            return carry

        lax.fori_loop(0, 16, tile, 0, unroll=8)

    def put_away(i):
        def put(y, rows, acc):
            sc[i, y, rows, :] = acc.astype(BF16)

        return put

    def put_own(i):
        def put(y, rows, acc):
            own[i, y, rows, :] = acc

        return put

    for i in ORDER:
        totals(i, 1 - core, put_away(i))
        if i == ORDER[0]:
            pl.semaphore_wait(barrier, len(peers))
        c_copy(i).start()
        totals(i, core, put_own(i))

    own_half = pl.ds(pl.multiple_of(half * 128, 128), 128)
    far_half = pl.ds(pl.multiple_of((1 - half) * 128, 128), 128)

    def y_copy(m, i):
        return remote(ys.at[m - 1, i], yr.at[m - 1, i], ysend.at[m - 1, i], yrecv.at[m - 1, i], y_peers[m])

    def both(i, y, rows):
        return own[i, y, rows, :] + cr[i, y, rows, :].astype(F32)

    for i in ORDER:
        c_copy(i).wait_recv()
        ys[2, i] = both(i, 1 - ylo, far_half).astype(BF16)
        y_copy(3, i).start()
        ys[1, i] = both(i, ylo, far_half).astype(BF16)
        y_copy(2, i).start()
        ys[0, i] = both(i, 1 - ylo, own_half).astype(BF16)
        y_copy(1, i).start()
        kept[i] = both(i, ylo, own_half)

    def z_copy(j, i):
        return remote(zs.at[j, i], zr.at[j, i], zsend.at[j, i], zrecv.at[j, i], z_peer)

    first = half == 0

    def near_sum(j, i):
        y_copy(1, i).wait_recv()
        zs[j, i] = (kept[i] + yr[0, i].astype(F32)).astype(BF16)

    def far_sum(j, i):
        y_copy(2, i).wait_recv()
        y_copy(3, i).wait_recv()
        zs[j, i] = (yr[1, i].astype(F32) + yr[2, i].astype(F32)).astype(BF16)

    for i in ORDER:
        @pl.when(first)
        def _():
            near_sum(0, i)

        @pl.when(jnp.logical_not(first))
        def _():
            far_sum(0, i)

        z_copy(0, i).start()

    for i in range(3):
        @pl.when(first)
        def _():
            far_sum(1, i)

        @pl.when(jnp.logical_not(first))
        def _():
            near_sum(1, i)

    loads[1].wait()
    f_copy = remote(fv.at[:, far_half], fx, fsend, frecv, y_peers[2])
    f_copy.start()

    top = pl.multiple_of(row * 256 + half * 128, 128)

    def rows_of(i):
        return pl.ds(top, 128) if i == 0 else pl.ds(OWN_ROWS + (i - 1) * 128, 128)

    for k in range(PANELS):
        @pl.when(row <= k)
        def _():
            l_st[k, rows_of(0), :] = jnp.zeros((128, 256), BF16)

    f_copy.wait_recv()

    def g_copy(m, i):
        ref = a_st.at[xpos, rows_of(i)]
        return remote(ref, ref, gsend.at[m - 1, i], grecv.at[m - 1, i], x_peers[m])

    def g_arrival(m, i):
        ref = a_st.at[xpos ^ m, rows_of(i)]
        return remote(ref, ref, gsend.at[m - 1, i], grecv.at[m - 1, i], x_peers[m])

    def critical(i):
        z_copy(0, i).wait_recv()
        base = jnp.where(first, fv[i, own_half, :].astype(F32), fx[i].astype(F32))
        a_st[xpos, rows_of(i), :] = (base + zr[0, i].astype(F32)).astype(BF16)

    def owner(m):
        return row ^ (2 * (m & 1)), half ^ (m >> 1)

    def tri_place(k, r, h):
        return a_st.at[k, pl.ds(pl.multiple_of(r * 256 + h * 128, 128), 128)]

    def lead_place(k, h):
        return a_st.at[k, pl.ds(pl.multiple_of(LEAD_ROWS + h * 128, 128), 128)]

    def t_copy(m, k):
        ref = tri_place(k, row, half)
        return remote(ref, ref, tsend.at[m - 1, k], trecv.at[m - 1, k], y_peers[m])

    def t_arrival(m, k):
        ref = tri_place(k, *owner(m))
        return remote(ref, ref, tsend.at[m - 1, k], trecv.at[m - 1, k], y_peers[m])

    def u_copy(m, k):
        ref = tri_place(k, *owner(m))
        return remote(ref, ref, usend.at[m, k], urecv.at[m, k], core_peer)

    def u_arrival(m, k):
        r, h = owner(m)
        ref = tri_place(k, r ^ 1, h)
        return remote(ref, ref, usend.at[m, k], urecv.at[m, k], core_peer)

    def q_copy(m, k):
        src = a_st.at[k, rows_of(1)]
        return remote(src, lead_place(k, half), qsend.at[m - 1, k], qrecv.at[m - 1, k], y_peers[m])

    def q_arrival(m, k):
        ref = lead_place(k, owner(m)[1])
        return remote(ref, ref, qsend.at[m - 1, k], qrecv.at[m - 1, k], y_peers[m])

    def v_copy(m, k):
        ref = lead_place(k, owner(m)[1])
        src = a_st.at[k, rows_of(1)] if m == 0 else ref
        return remote(src, ref, vsend.at[m, k], vrecv.at[m, k], core_peer)

    def each(count, body):
        def step(k, carry):
            body(k)
            return carry

        lax.fori_loop(0, count, step, 0)

    def send_lead(k):
        @pl.when(row == xpos)
        def _():
            for m in (3, 1, 2):
                q_copy(m, k).start()
            v_copy(0, k).start()

    def send_tri(k):
        @pl.when(row > k)
        def _():
            for m in (3, 1, 2):
                t_copy(m, k).start()
            u_copy(0, k).start()

    critical(1)
    for m in (1, 3, 2):
        g_copy(m, 1).start()
    send_lead(xpos)
    z_copy(1, 0).start()

    critical(0)

    @pl.when(row > xpos)
    def _():
        for m in (1, 3, 2):
            g_copy(m, 0).start()

    send_tri(xpos)
    z_copy(1, 1).start()

    for m in (1, 3, 2):
        g_arrival(m, 1).wait_recv()
        send_lead(xpos ^ m)

        @pl.when(row > (xpos ^ m))
        def _():
            g_arrival(m, 0).wait_recv()

        send_tri(xpos ^ m)

    @pl.when(row == xpos)
    def _():
        for k in range(4):
            a_st[k, pl.ds(pl.multiple_of(LEAD_ROWS + half * 128, 128), 128), :] = a_st[k, rows_of(1), :]

    critical(2)
    for m in (1, 3, 2):
        g_copy(m, 2).start()
    z_copy(1, 2).start()

    for n in (0, 1, 3, 2):
        k = xpos ^ n
        for m in (1, 3, 2):
            @pl.when(owner(m)[0] == xpos)
            def _():
                q_arrival(m, k).wait_recv()
                v_copy(m, k).start()

            @pl.when(owner(m)[0] > k)
            def _():
                t_arrival(m, k).wait_recv()
                u_copy(m, k).start()

    for m in range(4):
        each(owner(m)[0] ^ 1, lambda k: u_arrival(m, k).wait_recv())
    loads[2].wait()

    def panel(k, b):
        rows = pl.ds(b * 256, 256)
        acc = a_st[k, rows, :].astype(F32)
        for m in range(k):
            acc = acc - dot_t(l_st[m, rows, :], l_st[m, pl.ds(k * 256, 256), :])
        weight = wv[pl.ds(k * 256, 256), :]
        l_st[k, rows, :] = jnp.dot(acc.astype(BF16), weight, preferred_element_type=F32).astype(BF16)

    for k in range(3):
        for b in range(k + 1, 4):
            panel(k, b)
    for m in (1, 2, 3):
        g_arrival(m, 2).wait_recv()
    for k in range(PANELS):
        panel(k, 4)
    def o_copy(i):
        return remote(ox.at[i], out.at[i, own_half], osend.at[i], orecv.at[i], y_peers[2])

    def keep_copy(i):
        return pltpu.make_async_copy(ob.at[i], out.at[i, own_half], lsem.at[3 + i])

    def o_arrival(i):
        return remote(ox.at[i], out.at[i, far_half], osend.at[i], orecv.at[i], y_peers[2])

    for i in range(3):
        early = l_st[xpos, rows_of(i), :]

        @pl.when(first)
        def _():
            ob[i] = early
            keep_copy(i).start()

        @pl.when(jnp.logical_not(first))
        def _():
            ox[i] = early
            o_copy(i).start()

    for m in range(4):
        @pl.when((owner(m)[0] ^ 1) == xpos)
        def _():
            for k in range(4):
                v_copy(m, k).wait_recv()

    for k in range(PANELS):
        panel(k, 5)

    for i in range(3):
        acc = jnp.where(first, fx[i].astype(F32), fv[i, own_half, :].astype(F32))
        for k in range(PANELS):
            acc = acc - dot_t(l_st[k, rows_of(i), :], l_st[k, pl.ds(LEAD_ROWS, 256), :])
        z_copy(1, i).wait_recv()
        late = (acc + zr[1, i].astype(F32)).astype(BF16)

        @pl.when(first)
        def _():
            ox[i] = late
            o_copy(i).start()

        @pl.when(jnp.logical_not(first))
        def _():
            ob[i] = late
            keep_copy(i).start()

    for i in range(3):
        o_arrival(i).wait_recv()

    f_copy.wait_send()
    for i in range(3):
        c_copy(i).wait_send()
        o_copy(i).wait_send()
        for m in (1, 2, 3):
            y_copy(m, i).wait_send()
            if i:
                g_copy(m, i).wait_send()

    @pl.when(row > xpos)
    def _():
        for m in (1, 2, 3):
            g_copy(m, 0).wait_send()

    def drain_tri(k):
        for m in (1, 2, 3):
            t_copy(m, k).wait_send()

    each(row, drain_tri)
    for m in range(4):
        each(owner(m)[0], lambda k: u_copy(m, k).wait_send())

        @pl.when(owner(m)[0] == xpos)
        def _():
            for k in range(4):
                v_copy(m, k).wait_send()

    @pl.when(row == xpos)
    def _():
        for m in (1, 2, 3):
            for k in range(4):
                q_copy(m, k).wait_send()

    for i in range(3):
        for j in range(2):
            z_copy(j, i).wait_send()
    for i in range(3):
        keep_copy(i).wait()


def shards(front, panel_inverse, contrib, pattern, front_map):
    hbm = pl.BlockSpec(memory_space=pl.ANY)
    smem = pl.BlockSpec(memory_space=pltpu.SMEM)

    def vmem(*shape, dtype=BF16):
        return pltpu.VMEM(shape, dtype)

    def dma(*shape):
        return pltpu.SemaphoreType.DMA(shape)

    out = pl.pallas_call(
        kernel,
        out_shape=jax.ShapeDtypeStruct((3, 256, 256), BF16),
        in_specs=[hbm, hbm, hbm, smem, smem],
        out_specs=hbm,
        scratch_shapes=[
            vmem(6, 256, 256),
            vmem(3, 256, 256),
            vmem(1024, 256),
            vmem(3, 2, 256, 256),
            vmem(3, 2, 256, 256),
            vmem(3, 2, 256, 256, dtype=F32),
            vmem(3, 128, 256, dtype=F32),
            vmem(3, 3, 128, 256),
            vmem(3, 3, 128, 256),
            vmem(2, 3, 128, 256),
            vmem(2, 3, 128, 256),
            vmem(3, 128, 256),
            vmem(4, 1536, 256),
            vmem(4, 1536, 256),
            vmem(3, 128, 256),
            vmem(3, 128, 256),
            dma(6),
            dma(3), dma(3), dma(3, 3), dma(3, 3),
            pltpu.SemaphoreType.DMA, pltpu.SemaphoreType.DMA,
            dma(2, 3), dma(2, 3),
            dma(3, 3), dma(3, 3),
            dma(3, 3), dma(3, 3), dma(4, 3), dma(4, 3),
            dma(3, 4), dma(3, 4), dma(4, 4), dma(4, 4),
            dma(3), dma(3),
        ],
        compiler_params=pltpu.CompilerParams(
            collective_id=0, has_side_effects=True, vmem_limit_bytes=107 * 2**19
        ),
        name="extend_add_eliminate",
    )(front.reshape(3, 256, 256), panel_inverse[0], contrib[0], pattern[0].T, front_map[0])
    return out.reshape(1, 768, 256)


def solution(mesh):
    in_specs = (
        P("cube", "row", "col"),
        P("cube", None, None),
        P("cube", ("row", "col"), None, None),
        P("cube", ("row", "col"), None),
        P("cube", None),
    )
    out_specs = P("cube", "row", "col")
    return jax.shard_map(shards, mesh=mesh, in_specs=in_specs, out_specs=out_specs, check_vma=False)
```
